128 devices in a mesh: gx: 2 (over core), gy: 16 (over y, x), gz: 4 (over z).
Axes of the slice: x: 4, y: 4, z: 4, core: 2. Of those that a mesh axis runs over, the one named last changes fastest.
Arguments:
- field: float32 [512, 512, 1024], P('gx', 'gy', 'gz'), may hold values from -60 to 60
- start_one: float32 [512, 128], replicated, may hold values from -6 to 6
- start_two: float32 [512, 128], replicated, may hold values from -6 to 6
Outputs:
- basis_one: float32 [512, 128], P('gx')
- basis_two: float32 [512, 128], P('gy')
- core: float32 [128, 128, 1024], P('gx', 'gy', 'gz')
The draws below stay inside these ranges and needn't reach their ends.
All inputs are finite; a program needn't handle non-finite values.
Results may differ from the reference program's by a relative error of at most 0.00024.
Values sent between devices are 32-bit elements; how exact they have to be, the bound alone decides.
A program may use at most 128 MiB of HBM per device.

```python
import math
import jax
import jax.numpy as jnp
from jax import lax

N1 = 512
N2 = 512
NV = 16
RANK = 128
ITERS = 2
N3 = 64


def draw_field(key, part):
    key = jax.random.fold_in(key, 7)
    first_key, second_key, noise_key = jax.random.split(key, 3)
    noise = jnp.clip(jax.random.normal(noise_key, (N1, N2, N3 * NV), jnp.float32), -6.0, 6.0)
    spread = math.log(3.0)
    scale_first = jnp.exp(jax.random.uniform(first_key, (N1,), jnp.float32) * spread)
    scale_second = jnp.exp(jax.random.uniform(second_key, (N2,), jnp.float32) * spread)
    return noise * scale_first[:, None, None] * scale_second[None, :, None]


def gaussian(own_key, shape, scale, reach, kind=jnp.bfloat16):
    array = scale * jax.random.normal(own_key, shape, jnp.float32)
    return jnp.clip(array, min=-reach, max=reach).astype(kind)


def setup_inputs(seed: int = 0) -> dict:
    keys = jax.random.split(jax.random.key(seed), 4)
    return {
        "field": draw_field(jax.random.fold_in(keys[3], 71), 0),
        "start_one": gaussian(keys[1], (N1, RANK), 1.0, 6.0, jnp.float32),
        "start_two": gaussian(keys[2], (N2, RANK), 1.0, 6.0, jnp.float32),
    }


def orthonormal(matrix, start_basis):
    current = start_basis
    for step in range(ITERS):
        product = jnp.dot(matrix, current, precision=lax.Precision.HIGHEST)
        crossed = jnp.dot(product.T, product, precision=lax.Precision.HIGHEST)
        factor = jnp.linalg.cholesky(crossed)
        current = jax.scipy.linalg.solve_triangular(factor, product.T, lower=True).T
    return current

def reference(field, start_one, start_two):
    unfolded = field.reshape(N1, -1)
    gram_one = jnp.dot(unfolded, unfolded.T, precision=lax.Precision.HIGHEST)
    basis_one = orthonormal(gram_one, start_one)
    projected = jnp.dot(basis_one.T, unfolded, precision=lax.Precision.HIGHEST).reshape(RANK, N2, N3 * NV)
    gram_two = lax.dot_general(projected, projected, (((0, 2), (0, 2)), ((), ())), precision=lax.Precision.HIGHEST)
    basis_two = orthonormal(gram_two, start_two)
    core = jnp.einsum('js,rjm->rsm', basis_two, projected, precision=lax.Precision.HIGHEST)
    return (basis_one, basis_two, core)
```

```python
import functools

import jax
import jax.numpy as jnp
from jax import lax
from jax.experimental import pallas as pl
from jax.experimental.pallas import tpu as pltpu
from jax.sharding import PartitionSpec as P

RANK = 128
ITERS = 2
MESH = pl.DeviceIdType.MESH
f32 = jnp.float32
bf16 = jnp.bfloat16
highest = lax.Precision.HIGHEST
VMEM_LIMIT = 56 * 1024 * 1024


def split(value):
    high = value.astype(bf16)
    return high, (value - high.astype(f32)).astype(bf16)


def dot_nt(a, b, precision=None):
    return lax.dot_general(a, b, (((1,), (1,)), ((), ())), precision=precision, preferred_element_type=f32)


def dot_tn(a, b, precision=None):
    return lax.dot_general(a, b, (((0,), (0,)), ((), ())), precision=precision, preferred_element_type=f32)


def dot_nn(a, b, precision=None):
    return lax.dot_general(a, b, (((1,), (0,)), ((), ())), precision=precision, preferred_element_type=f32)


class Place:
    def __init__(self, plane):
        self.gx, self.gy, self.gz = (lax.axis_index(name) for name in ("gx", "gy", "gz"))
        self.partner = 1 - self.gx
        self.ny, self.nx, self.nz = plane
        self.np = self.ny * self.nx
        self.y, self.x = self.gy // self.nx, self.gy % self.nx

    def plane_peer(self, d):
        dy, dx = d // self.nx, d % self.nx
        return (self.y + dy) % self.ny * self.nx + (self.x + dx) % self.nx

    def z_peer(self, d):
        return (self.gz + d) % self.nz

    def others(self, kinds):
        found = []
        if "x" in kinds:
            found.append({"gx": self.partner})
        if "p" in kinds:
            found += [{"gy": self.plane_peer(d)} for d in range(1, self.np)]
        if "z" in kinds:
            found += [{"gz": self.z_peer(d)} for d in range(1, self.nz)]
        return found

    def barrier(self, kinds):
        sem = pltpu.get_barrier_semaphore()
        peers = self.others(kinds)
        for peer in peers:
            pl.semaphore_signal(sem, inc=1, device_id=peer, device_id_type=MESH)
        pl.semaphore_wait(sem, len(peers))


def remote(src, dst, send_sem, recv_sem, device_id):
    copy = pltpu.make_async_remote_copy(
        src_ref=src, dst_ref=dst, send_sem=send_sem, recv_sem=recv_sem, device_id=device_id, device_id_type=MESH
    )
    copy.start()
    return copy


def sum_scratch(plane, rows, width):
    ny, nx, nz = plane
    planes = ny * nx
    chunk = rows // planes
    dma = pltpu.SemaphoreType.DMA
    return [
        pltpu.VMEM((rows, width), f32),
        pltpu.VMEM((planes, chunk, width), f32),
        pltpu.VMEM((nz, chunk, width), f32),
        pltpu.VMEM((2, rows, width), f32),
        dma((2, planes)),
        dma((2, nz)),
        dma((2, planes)),
        dma((2,)),
    ]


def sum_over_chips(place, total, parts, zparts, whole, rs_sem, z_sem, ag_sem, x_sem):
    rows, width = total.shape
    chunk = rows // place.np
    copies = []
    for d in range(1, place.np):
        peer = place.plane_peer(d)
        copies.append(
            remote(
                total.at[pl.ds(pl.multiple_of(peer * chunk, 8), chunk), :],
                parts.at[d],
                rs_sem.at[0, d],
                rs_sem.at[1, d],
                {"gy": peer},
            )
        )
    own = pl.ds(pl.multiple_of(place.gy * chunk, 8), chunk)
    value = total[own, :]
    for d, copy in enumerate(copies, 1):
        copy.wait_recv()
        value = value + parts[d]
    zparts[place.gz] = value
    for copy in copies:
        copy.wait_send()
    copies = [
        remote(
            zparts.at[place.gz], zparts.at[place.gz], z_sem.at[0, d], z_sem.at[1, d], {"gz": place.z_peer(d)}
        )
        for d in range(1, place.nz)
    ]
    for copy in copies:
        copy.wait_recv()
    value = zparts[0]
    for z in range(1, place.nz):
        value = value + zparts[z]
    whole[place.gx, own, :] = value
    for copy in copies:
        copy.wait_send()
    block = whole.at[place.gx, own, :]
    copies = [
        remote(block, block, ag_sem.at[0, d], ag_sem.at[1, d], {"gy": place.plane_peer(d)})
        for d in range(1, place.np)
    ]
    for copy in copies:
        copy.wait_recv()
    mine = whole.at[place.gx]
    last = remote(mine, mine, x_sem.at[0], x_sem.at[1], {"gx": place.partner})
    for copy in copies:
        copy.wait_send()
    last.wait()


def unfold_sum(whole, gram_ref):
    half = whole.shape[2]
    quarter = half // 2
    gram_ref[0:half, 0:half] = whole[0, 0:half, :]
    gram_ref[half:, half:] = whole[1, 0:half, :]
    upper = jnp.concatenate([whole[0, half:, :], whole[1, half:, :]], axis=0)
    gram_ref[0:half, half:] = upper
    gram_ref[half:, 0:half] = upper.T


def load_field(field, own, load_sem):
    loads = []
    for c in range(field.shape[1] // 8):
        at = slice(8 * c, 8 * c + 8)
        loads.append([])
        for h in range(field.shape[2] // 128):
            lanes = slice(128 * h, 128 * h + 128)
            loads[c].append(pltpu.make_async_copy(field.at[:, at, lanes], own.at[h, :, at, :], load_sem.at[c, h]))
            loads[c][h].start()
    return loads


def take(block, j):
    halves, rows, cols, lanes = block.shape
    flat = block.reshape(halves * rows * cols, lanes)
    return jnp.concatenate([flat[pl.ds(h * rows * cols + j, rows, stride=cols), :] for h in range(halves)], axis=1)


def split_rows(block, high, low, c):
    depth = block.shape[0] * 128
    for j in range(8 * c, 8 * c + 8):
        at = slice(j * depth, (j + 1) * depth)
        high[:, at], low[:, at] = split(take(block, j))


def gram_one_kernel(
    plane, field, gram_ref, own, other, high, low, high_p, low_p, acc, mixed, cross, crossed, load_sem, field_sem, cross_sem, *sums
):
    place = Place(plane)
    rows, cols, depth = field.shape
    half = cols // 2
    blocks = cols // 8
    gx, partner = place.gx, place.partner
    place.barrier("xpz")
    sends = []
    for c in range(blocks // 2):
        for h in range(depth // 128):
            sends.append(
                remote(
                    field.at[:, pl.ds(pl.multiple_of(partner * half + 8 * c, 8), 8), 128 * h : 128 * h + 128],
                    other.at[h, :, 8 * c : 8 * c + 8, :],
                    field_sem.at[0, c, h],
                    field_sem.at[1, c, h],
                    {"gx": partner},
                )
            )
    loads = load_field(field, own, load_sem)
    acc[...] = jnp.zeros_like(acc)
    mixed[...] = jnp.zeros_like(mixed)
    cross[...] = jnp.zeros_like(cross)
    for c in range(blocks):
        for load in loads[c]:
            load.wait()
        split_rows(own, high, low, c)
        at = slice(8 * c * depth, 8 * (c + 1) * depth)
        acc[...] += dot_nt(high[:, at], high[:, at])
        mixed[...] += dot_nt(high[:, at], low[:, at])
    for c in range(blocks // 2):
        for h in range(depth // 128):
            sends[c * (depth // 128) + h].wait_recv()
        split_rows(other, high_p, low_p, c)
        at = slice(8 * c * depth, 8 * (c + 1) * depth)
        mine = pl.ds(pl.multiple_of((gx * half + 8 * c) * depth, 8 * depth), 8 * depth)
        cross[...] += dot_nt(high[:, mine], high_p[:, at])
        cross[...] += dot_nt(high[:, mine], low_p[:, at])
        cross[...] += dot_nt(low[:, mine], high_p[:, at])
    value = cross[...]
    cross[...] = jnp.where(gx == 0, value, value.T)
    quarter = rows // 2
    copy = remote(
        cross.at[pl.ds(pl.multiple_of(partner * quarter, 8), quarter), :],
        crossed,
        cross_sem.at[0],
        cross_sem.at[1],
        {"gx": partner},
    )
    total = sums[0]
    total[0:rows, :] = acc[...] + mixed[...] + mixed[...].T
    copy.wait_recv()
    total[rows:, :] = cross[pl.ds(pl.multiple_of(gx * quarter, 8), quarter), :] + crossed[...]
    sum_over_chips(place, *sums)
    copy.wait_send()
    for send in sends:
        send.wait_send()
    unfold_sum(sums[3], gram_ref)


def gram_one_call(plane, field):
    rows, cols, depth = field.shape
    dma = pltpu.SemaphoreType.DMA
    return pl.pallas_call(
        functools.partial(gram_one_kernel, plane),
        out_shape=jax.ShapeDtypeStruct((2 * rows, 2 * rows), f32),
        in_specs=[pl.BlockSpec(memory_space=pl.ANY)],
        out_specs=pl.BlockSpec(memory_space=pltpu.VMEM),
        scratch_shapes=[
            pltpu.VMEM((depth // 128, rows, cols, 128), f32),
            pltpu.VMEM((depth // 128, rows, cols // 2, 128), f32),
            pltpu.VMEM((rows, cols * depth), bf16),
            pltpu.VMEM((rows, cols * depth), bf16),
            pltpu.VMEM((rows, cols // 2 * depth), bf16),
            pltpu.VMEM((rows, cols // 2 * depth), bf16),
            pltpu.VMEM((rows, rows), f32),
            pltpu.VMEM((rows, rows), f32),
            pltpu.VMEM((rows, rows), f32),
            pltpu.VMEM((rows // 2, rows), f32),
            dma((cols // 8, depth // 128)),
            dma((2, cols // 16, depth // 128)),
            dma((2,)),
            *sum_scratch(plane, rows * 3 // 2, rows),
        ],
        compiler_params=pltpu.CompilerParams(collective_id=0, has_side_effects=True, vmem_limit_bytes=VMEM_LIMIT),
        name="gram_one",
    )(field)


def inverse_factor(crossed):
    n = crossed.shape[0]
    row_of = lax.broadcasted_iota(jnp.int32, (8, n), 0)
    col_of = lax.broadcasted_iota(jnp.int32, (8, n), 1)
    left = [crossed[8 * t : 8 * t + 8, :] for t in range(n // 8)]
    right = [jnp.where(col_of == row_of + 8 * t, 1.0, 0.0).astype(f32) for t in range(n // 8)]
    down = lax.broadcasted_iota(jnp.int32, (8, 1), 0)
    scales = [jnp.zeros((8, 1), f32) for _ in range(n // 8)]
    for k in range(n):
        t, s = divmod(k, 8)
        row, beside = left[t][s : s + 1, :], right[t][s : s + 1, :]
        pivot = row[:, k : k + 1]
        scales[t] = jnp.where(down == s, lax.rsqrt(pivot), scales[t])
        row, beside = row / pivot, beside / pivot
        for u in range(t, n // 8):
            factor = left[u][:, k : k + 1]
            if u == t:
                factor = jnp.where(down > s, factor, 0.0)
            left[u] = left[u] - factor * row
            right[u] = right[u] - factor * beside
    return jnp.concatenate([right[t] * scales[t] for t in range(n // 8)], axis=0)


def orth_kernel(axis, gram, start, whole_ref, own_ref):
    value = start[...]
    for _ in range(ITERS):
        product = dot_nn(gram[...], value, highest)
        crossed = dot_tn(product, product, highest)
        value = dot_nt(product, inverse_factor(crossed), highest)
    whole_ref[...] = value
    rows = own_ref.shape[0]
    own_ref[...] = whole_ref[pl.ds(pl.multiple_of(lax.axis_index(axis) * rows, 8), rows), :]


def orth_call(axis, own_rows, gram, start):
    vmem = pl.BlockSpec(memory_space=pltpu.VMEM)
    return pl.pallas_call(
        functools.partial(orth_kernel, axis),
        out_shape=(jax.ShapeDtypeStruct(start.shape, f32), jax.ShapeDtypeStruct((own_rows, RANK), f32)),
        in_specs=[vmem, vmem],
        out_specs=(vmem, vmem),
        compiler_params=pltpu.CompilerParams(vmem_limit_bytes=VMEM_LIMIT),
        name="orth_" + axis,
    )(gram, start)


def project_kernel(
    plane, field, basis, gram_ref, kept_ref, own, partial, arrived, projected, kept, high, low, mixed, halves, crossed,
    load_sem, pair_sem, trade_sem, cross_sem, *sums
):
    place = Place(plane)
    rows, cols, depth = field.shape
    blocks = cols // 8
    gx, gy, partner = place.gx, place.gy, place.partner
    ranks = RANK // 2
    part_ranks = kept.shape[1]
    part_depth = kept.shape[2]
    splits = depth // part_depth
    loads = load_field(field, own, load_sem)
    place.barrier("xpz")
    basis_high, basis_low = split(basis[pl.ds(pl.multiple_of(gx * rows, 8), rows), :].T)
    both = jnp.concatenate([basis_high, basis_low], axis=0)
    pairs = []
    for c in range(blocks):
        for load in loads[c]:
            load.wait()
        for j in range(8 * c, 8 * c + 8):
            field_high, field_low = split(take(own, j))
            first = dot_nn(both, field_high)
            partial[j] = first[:RANK] + first[RANK:] + dot_nn(basis_high, field_low)
        pairs.append(
            remote(
                partial.at[8 * c : 8 * c + 8, pl.ds(pl.multiple_of(partner * ranks, 8), ranks), :],
                arrived.at[8 * c : 8 * c + 8],
                pair_sem.at[0, c],
                pair_sem.at[1, c],
                {"gx": partner},
            )
        )
    here = pl.ds(pl.multiple_of(gx * ranks, 8), ranks)
    for c in range(blocks):
        pairs[c].wait_recv()
        for j in range(8 * c, 8 * c + 8):
            projected[j] = partial[j, here, :] + arrived[j]

    def piece(peer):
        return projected.at[
            :,
            pl.ds(pl.multiple_of(peer // splits * part_ranks, 8), part_ranks),
            pl.ds(pl.multiple_of(peer % splits * part_depth, 128), part_depth),
        ]

    landing = kept.at[pl.ds(gy * cols, cols), :, :]
    trades = []
    for d in range(1, place.np):
        peer = place.plane_peer(d)
        trades.append(remote(piece(peer), landing, trade_sem.at[0, d], trade_sem.at[1, d], {"gy": peer}))
    local = pltpu.make_async_copy(piece(gy), landing, trade_sem.at[0, 0])
    local.start()
    local.wait()
    for trade in trades:
        trade.wait_recv()
    whole_rows = cols * place.np
    half = whole_rows // 2
    kept_rows = kept.reshape(whole_rows * part_ranks, part_depth)
    for r in range(part_ranks):
        at = slice(r * part_depth, (r + 1) * part_depth)
        high[:, at], low[:, at] = split(kept_rows[pl.ds(r, whole_rows, stride=part_ranks), :])
    top, bottom = slice(0, half), slice(half, whole_rows)
    for k, at in enumerate((top, bottom)):
        mixed[...] = dot_nt(high[at, :], low[at, :])
        halves[k, 0:half, :] = dot_nt(high[at, :], high[at, :])
        halves[k, 0:half, :] += mixed[...] + mixed[...].T
    cross = dot_nt(high[top, :], high[bottom, :])
    cross += dot_nt(high[top, :], low[bottom, :])
    cross += dot_nt(low[top, :], high[bottom, :])
    halves[0, half:, :] = cross[: half // 2]
    halves[1, half:, :] = cross[half // 2 :]
    copy = remote(halves.at[partner], crossed, cross_sem.at[0], cross_sem.at[1], {"gx": partner})
    copy.wait_recv()
    sums[0][...] = halves[gx] + crossed[...]
    sum_over_chips(place, *sums)
    copy.wait_send()
    for send in pairs + trades:
        send.wait_send()
    unfold_sum(sums[3], gram_ref)
    kept_ref[...] = kept[...]


def project_call(plane, field, basis):
    rows, cols, depth = field.shape
    ny, nx, nz = plane
    planes = ny * nx
    splits = depth // 128
    part_ranks = RANK // 2 // (planes // splits)
    whole_rows = planes * cols
    half = whole_rows // 2
    dma = pltpu.SemaphoreType.DMA
    kept_shape = (whole_rows, part_ranks, depth // splits)
    vmem = pl.BlockSpec(memory_space=pltpu.VMEM)
    return pl.pallas_call(
        functools.partial(project_kernel, plane),
        out_shape=(jax.ShapeDtypeStruct((whole_rows, whole_rows), f32), jax.ShapeDtypeStruct(kept_shape, f32)),
        in_specs=[pl.BlockSpec(memory_space=pl.ANY), vmem],
        out_specs=(vmem, vmem),
        scratch_shapes=[
            pltpu.VMEM((depth // 128, rows, cols, 128), f32),
            pltpu.VMEM((cols, RANK, depth), f32),
            pltpu.VMEM((cols, RANK // 2, depth), f32),
            pltpu.VMEM((cols, RANK // 2, depth), f32),
            pltpu.VMEM(kept_shape, f32),
            pltpu.VMEM((whole_rows, part_ranks * 128), bf16),
            pltpu.VMEM((whole_rows, part_ranks * 128), bf16),
            pltpu.VMEM((half, half), f32),
            pltpu.VMEM((2, half * 3 // 2, half), f32),
            pltpu.VMEM((half * 3 // 2, half), f32),
            dma((cols // 8, depth // 128)),
            dma((2, cols // 8)),
            dma((2, planes)),
            dma((2,)),
            *sum_scratch(plane, half * 3 // 2, half),
        ],
        compiler_params=pltpu.CompilerParams(collective_id=1, has_side_effects=True, vmem_limit_bytes=VMEM_LIMIT),
        name="project",
    )(field, basis)


def core_kernel(plane, kept, basis, core_ref, parts, landed, trade_sem):
    place = Place(plane)
    gy = place.gy
    whole_rows, part_ranks, part_depth = kept.shape
    ranks, cols, depth = landed.shape
    splits = depth // part_depth
    place.barrier("p")
    basis_high, basis_low = split(basis[...].T)
    both = jnp.concatenate([basis_high, basis_low], axis=0)
    kept_rows = kept.reshape(whole_rows * part_ranks, part_depth)
    for r in range(part_ranks):
        high, low = split(kept_rows[pl.ds(r, whole_rows, stride=part_ranks), :])
        first = dot_nn(both, high)
        parts[r] = first[:RANK] + first[RANK:] + dot_nn(basis_high, low)
    landing = landed.at[
        pl.ds(gy // splits * part_ranks, part_ranks),
        :,
        pl.ds(pl.multiple_of(gy % splits * part_depth, 128), part_depth),
    ]

    def piece(peer):
        return parts.at[:, pl.ds(pl.multiple_of(peer * cols, 8), cols), :]

    trades = []
    for d in range(1, place.np):
        peer = place.plane_peer(d)
        trades.append(remote(piece(peer), landing, trade_sem.at[0, d], trade_sem.at[1, d], {"gy": peer}))
    local = pltpu.make_async_copy(piece(gy), landing, trade_sem.at[0, 0])
    local.start()
    local.wait()
    for trade in trades:
        trade.wait_recv()
    core_ref[...] = landed[...]
    for trade in trades:
        trade.wait_send()


def core_call(plane, kept, basis, depth):
    ny, nx, nz = plane
    planes = ny * nx
    whole_rows, part_ranks, part_depth = kept.shape
    shape = (RANK // 2, RANK // planes, depth)
    vmem = pl.BlockSpec(memory_space=pltpu.VMEM)
    return pl.pallas_call(
        functools.partial(core_kernel, plane),
        out_shape=jax.ShapeDtypeStruct(shape, f32),
        in_specs=[vmem, vmem],
        out_specs=vmem,
        scratch_shapes=[
            pltpu.VMEM((part_ranks, RANK, part_depth), f32),
            pltpu.VMEM(shape, f32),
            pltpu.SemaphoreType.DMA((2, planes)),
        ],
        compiler_params=pltpu.CompilerParams(collective_id=2, has_side_effects=True, vmem_limit_bytes=VMEM_LIMIT),
        name="core",
    )(kept, basis)


def body(plane, field, start_one, start_two):
    rows, cols, depth = field.shape
    gram_one = gram_one_call(plane, field)
    basis_one, own_one = orth_call("gx", rows, gram_one, start_one)
    gram_two, kept = project_call(plane, field, basis_one)
    basis_two, own_two = orth_call("gy", cols, gram_two, start_two)
    core = core_call(plane, kept, basis_two, depth)
    return (own_one, own_two, core)


def solution(mesh):
    sizes = dict(mesh.shape)
    side = 4 if sizes["gy"] == 16 else 2
    plane = (sizes["gy"] // side, side, sizes["gz"])
    return jax.shard_map(
        functools.partial(body, plane),
        mesh=mesh,
        in_specs=(P("gx", "gy", "gz"), P(), P()),
        out_specs=(P("gx", None), P("gy", None), P("gx", "gy", "gz")),
        check_vma=False,
    )
```

```python
import functools

import jax
import jax.numpy as jnp
from jax import lax
from jax.experimental import pallas as pl
from jax.experimental.pallas import tpu as pltpu
from jax.sharding import PartitionSpec as P

RANK = 128
ITERS = 2
MESH = pl.DeviceIdType.MESH
f32 = jnp.float32
bf16 = jnp.bfloat16
highest = lax.Precision.HIGHEST
VMEM_LIMIT = 56 * 1024 * 1024


def split(value):
    high = value.astype(bf16)
    return high, (value - high.astype(f32)).astype(bf16)


def dot_nt(a, b, precision=None):
    return lax.dot_general(a, b, (((1,), (1,)), ((), ())), precision=precision, preferred_element_type=f32)


def dot_tn(a, b, precision=None):
    return lax.dot_general(a, b, (((0,), (0,)), ((), ())), precision=precision, preferred_element_type=f32)


def dot_nn(a, b, precision=None):
    return lax.dot_general(a, b, (((1,), (0,)), ((), ())), precision=precision, preferred_element_type=f32)


class Place:
    def __init__(self, plane):
        self.gx, self.gy, self.gz = (lax.axis_index(name) for name in ("gx", "gy", "gz"))
        self.partner = 1 - self.gx
        self.ny, self.nx, self.nz = plane
        self.np = self.ny * self.nx
        self.y, self.x = self.gy // self.nx, self.gy % self.nx

    def plane_peer(self, d):
        dy, dx = d // self.nx, d % self.nx
        return (self.y + dy) % self.ny * self.nx + (self.x + dx) % self.nx

    def plane_source(self, d):
        dy, dx = d // self.nx, d % self.nx
        return (self.y - dy) % self.ny * self.nx + (self.x - dx) % self.nx

    def plane_order(self):
        def hops(d):
            dy, dx = d // self.nx, d % self.nx
            return min(dy, self.ny - dy) + min(dx, self.nx - dx)

        return sorted(range(1, self.np), key=lambda d: (-hops(d), d))

    def z_peer(self, d):
        return (self.gz + d) % self.nz

    def others(self, kinds):
        found = []
        if "x" in kinds:
            found.append({"gx": self.partner})
        if "p" in kinds:
            found += [{"gy": self.plane_peer(d)} for d in range(1, self.np)]
        if "z" in kinds:
            found += [{"gz": self.z_peer(d)} for d in range(1, self.nz)]
        return found

    def greet(self):
        for peer in self.others("pzx"):
            pl.semaphore_signal(pltpu.get_barrier_semaphore(), inc=1, device_id=peer, device_id_type=MESH)

    def meet(self):
        pl.semaphore_wait(pltpu.get_barrier_semaphore(), len(self.others("pzx")))


def remote(src, dst, send_sem, recv_sem, device_id):
    copy = pltpu.make_async_remote_copy(
        src_ref=src, dst_ref=dst, send_sem=send_sem, recv_sem=recv_sem, device_id=device_id, device_id_type=MESH
    )
    copy.start()
    return copy


def sum_scratch(plane, rows, width):
    ny, nx, nz = plane
    planes = ny * nx
    chunk = rows // planes
    dma = pltpu.SemaphoreType.DMA
    return [
        pltpu.VMEM((rows, width), f32),
        pltpu.VMEM((planes, chunk, width), f32),
        pltpu.VMEM((nz, chunk, width), f32),
        pltpu.VMEM((2, rows, width), f32),
        dma((2, planes)),
        dma((2, nz)),
        dma((2, planes)),
        dma((2,)),
    ]


def sum_over_chips(place, total, parts, zparts, whole, rs_sem, z_sem, ag_sem, x_sem):
    chunk = total.shape[0] // place.np
    order = place.plane_order()
    sent = []
    for d in order:
        peer = place.plane_peer(d)
        piece = total.at[pl.ds(pl.multiple_of(peer * chunk, 8), chunk), :]
        sent.append(remote(piece, parts.at[d], rs_sem.at[0, d], rs_sem.at[1, d], {"gy": peer}))
    own = pl.ds(pl.multiple_of(place.gy * chunk, 8), chunk)
    value = total[own, :]
    for d, copy in list(zip(order, sent))[::-1]:
        copy.wait_recv()
        value = value + parts[d]
    zparts[place.gz] = value
    mine = zparts.at[place.gz]
    copies = [
        remote(mine, mine, z_sem.at[0, d], z_sem.at[1, d], {"gz": place.z_peer(d)})
        for d in sorted(range(1, place.nz), key=lambda d: -min(d, place.nz - d))
    ]
    for copy in copies:
        copy.wait_recv()
    value = zparts[0]
    for z in range(1, place.nz):
        value = value + zparts[z]
    whole[place.gx, own, :] = value
    sent += copies
    block = whole.at[place.gx, own, :]
    copies = [remote(block, block, ag_sem.at[0, d], ag_sem.at[1, d], {"gy": place.plane_peer(d)}) for d in order]
    for copy in copies:
        copy.wait_recv()
    mine = whole.at[place.gx]
    last = remote(mine, mine, x_sem.at[0], x_sem.at[1], {"gx": place.partner})
    for copy in sent + copies:
        copy.wait_send()
    last.wait()


def unfold_sum(whole, gram):
    half = whole.shape[2]
    gram[0:half, 0:half] = whole[0, 0:half, :]
    gram[half:, half:] = whole[1, 0:half, :]
    upper = jnp.concatenate([whole[0, half:, :], whole[1, half:, :]], axis=0)
    gram[0:half, half:] = upper
    gram[half:, 0:half] = upper.T


def inverse_factor(crossed):
    n = crossed.shape[0]
    sub = lax.broadcasted_iota(jnp.int32, (8, n), 0)
    lane = lax.broadcasted_iota(jnp.int32, (8, n), 1)
    tiles = [crossed[8 * t : 8 * t + 8, :] for t in range(n // 8)]
    found = []

    def lanes_of(tile, k):
        return jnp.broadcast_to(tile[:, k : k + 1], (8, n))

    def rows_of(tile, k):
        return jnp.broadcast_to(tile[k : k + 1, :], (8, n))

    for t in range(n // 8):
        first = 8 * t
        inside = (lane >= first) & (lane < first + 8)
        columns = [lanes_of(tiles[t], first + k) for k in range(8)]
        block = jnp.where(inside, jnp.where(lane == sub + first, 1.0, 0.0), tiles[t])
        rows = jnp.zeros((8, n), f32)
        for k in range(0, 8, 2):
            one, two = sub == k, sub == k + 1
            fa, fb = columns[k], columns[k + 1]
            a, b, c = rows_of(fa, k), rows_of(fa, k + 1), rows_of(fb, k + 1)
            det = a * c - b * b
            inv = 1.0 / det
            ia, ib, ic = c * inv, b * inv, a * inv
            inv_a = 1.0 / a
            ratio = b * inv_a
            scale_one = lax.rsqrt(a)
            scale_two = lax.rsqrt(det * inv_a)

            def step(value, k=k, fa=fa, fb=fb, ia=ia, ib=ib, ic=ic, one=one, two=two):
                p, q = rows_of(value, k), rows_of(value, k + 1)
                zp, zq = ia * p - ib * q, ic * q - ib * p
                return p, q, jnp.where(one, zp, jnp.where(two, zq, value - fa * zp - fb * zq))

            p, q, block = step(block)
            rows = jnp.where(one, p * scale_one, jnp.where(two, (q - ratio * p) * scale_two, rows))
            for j in range(k + 2, 8):
                columns[j] = step(columns[j])[2]
        found.append(jnp.where(lane < first + 8, rows, 0.0))
        spread = [rows_of(block, k) for k in range(8)]
        for u in range(t + 1, n // 8):
            value = jnp.where(inside, 0.0, tiles[u])
            terms = [lanes_of(tiles[u], first + k) * spread[k] for k in range(8)]
            while len(terms) > 1:
                terms = [a + b for a, b in zip(terms[::2], terms[1::2])]
            tiles[u] = value - terms[0]
    return jnp.concatenate(found, axis=0)


def orthonormal(gram, value):
    for _ in range(ITERS):
        product = dot_nn(gram[...], value, highest)
        crossed = dot_tn(product, product, highest)
        value = dot_nt(product, inverse_factor(crossed), highest)
    return value


def split_block(block, at, pair):
    rows = block.shape[0]
    pair[0:rows, at], pair[rows:, at] = split(block)


def gram_one_sums(place, field, own, other, pair, pair_p, gram, cross, crossed, load_sem, field_sem, cross_sem, total):
    rows, cols, depth = field.shape
    half = cols // 2
    gx, partner = place.gx, place.partner
    step = 8 * depth
    loads = []
    for j in range(cols):
        loads.append(pltpu.make_async_copy(field.at[:, j, :], own.at[j], load_sem.at[j]))
        loads[-1].start()
    place.meet()
    sends = []
    for j in range(half):
        sends.append(
            remote(
                field.at[:, partner * half + j, :], other.at[j], field_sem.at[0, j], field_sem.at[1, j], {"gx": partner}
            )
        )
    gram[...] = jnp.zeros_like(gram)
    for c in range(cols // 8):
        for j in range(8 * c, 8 * c + 8):
            loads[j].wait()
            split_block(own[j], slice(j * depth, (j + 1) * depth), pair)
        at = slice(c * step, (c + 1) * step)
        gram[...] += dot_nt(pair[:, at], pair[0:rows, at])
    cross[...] = jnp.zeros_like(cross)
    for c in range(half // 8):
        for j in range(8 * c, 8 * c + 8):
            sends[j].wait_recv()
            split_block(other[j], slice(j * depth, (j + 1) * depth), pair_p)
        at = slice(c * step, (c + 1) * step)
        mine = pl.ds(pl.multiple_of(gx * half * depth + c * step, step), step)
        both = dot_nt(pair[:, mine], pair_p[0:rows, at])
        cross[...] += both[0:rows] + both[rows:] + dot_nt(pair[0:rows, mine], pair_p[rows:, at])
    value = cross[...]
    cross[...] = jnp.where(gx == 0, value, value.T)
    quarter = rows // 2
    copy = remote(
        cross.at[pl.ds(pl.multiple_of(partner * quarter, 8), quarter), :],
        crossed,
        cross_sem.at[0],
        cross_sem.at[1],
        {"gx": partner},
    )
    total[0:rows, :] = gram[0:rows, :] + gram[rows:, :] + gram[rows:, :].T
    copy.wait_recv()
    total[rows:, :] = cross[pl.ds(pl.multiple_of(gx * quarter, 8), quarter), :] + crossed[...]
    return sends + [copy]


def project(place, pair, basis, partial, arrived, projected, kept, pair_sem, trade_sem, cols, depth):
    gx, gy, partner = place.gx, place.gy, place.partner
    rows = pair.shape[0] // 2
    ranks = RANK // 2
    parts = trade_sem.shape[1]
    each = cols // parts
    _, part_ranks, part_depth = kept.shape
    splits = depth // part_depth
    basis_high, basis_low = split(basis[pl.ds(pl.multiple_of(gx * rows, 8), rows), :].T)
    both = jnp.concatenate([basis_high, basis_low], axis=0)
    here = pl.ds(pl.multiple_of(gx * ranks, 8), ranks)
    there = pl.ds(pl.multiple_of(partner * ranks, 8), ranks)

    def piece(q, peer):
        return projected.at[
            each * q : each * (q + 1),
            pl.ds(pl.multiple_of(peer // splits * part_ranks, 8), part_ranks),
            pl.ds(pl.multiple_of(peer % splits * part_depth, 128), part_depth),
        ]

    def landing(q):
        return kept.at[pl.ds(gy * cols + each * q, each), :, :]

    def partials(q):
        for j in range(each * q, each * (q + 1)):
            at = slice(j * depth, (j + 1) * depth)
            first = dot_nn(both, pair[0:rows, at])
            partial[j] = first[:RANK] + first[RANK:] + dot_nn(basis_high, pair[rows:, at])
        at = slice(each * q, each * (q + 1))
        return remote(partial.at[at, there, :], arrived.at[at], pair_sem.at[0, q], pair_sem.at[1, q], {"gx": partner})

    order = place.plane_order()
    pairs, trades = [partials(0)], {}
    for q in range(parts):
        if q + 1 < parts:
            pairs.append(partials(q + 1))
        pairs[q].wait_recv()
        for j in range(each * q, each * (q + 1)):
            projected[j] = partial[j, here, :] + arrived[j]
        for d in order:
            peer = place.plane_peer(d)
            trades[q, d] = remote(
                piece(q, peer), landing(q), trade_sem.at[0, q, d], trade_sem.at[1, q, d], {"gy": peer}
            )
    local = []
    for q in range(parts):
        local.append(pltpu.make_async_copy(piece(q, gy), landing(q), trade_sem.at[0, q, 0]))
        local[-1].start()
    return pairs, trades, local


def spread_kept(place, kept, kept_pair, peer, cols):
    whole_rows, part_ranks, lanes = kept.shape
    flat = kept.reshape(whole_rows * part_ranks, lanes)
    for r in range(part_ranks):
        value = flat[pl.ds(peer * cols * part_ranks + r, cols, stride=part_ranks), :]
        at = slice(r * lanes, (r + 1) * lanes)
        first = pl.ds(pl.multiple_of(peer * cols, 16), cols)
        second = pl.ds(pl.multiple_of(whole_rows + peer * cols, 16), cols)
        kept_pair[first, at], kept_pair[second, at] = split(value)


def gram_two_sums(place, kept_pair, gram, halves, crossed, cross_sem, total):
    whole_rows = kept_pair.shape[0] // 2
    half = whole_rows // 2
    for k in range(2):
        high = kept_pair[half * k : half * (k + 1), :]
        low = kept_pair[whole_rows + half * k : whole_rows + half * (k + 1), :]
        gram[...] = dot_nt(low, high)
        halves[k, 0:half, :] = dot_nt(high, high)
        halves[k, 0:half, :] += gram[...] + gram[...].T
    high, low = kept_pair[0:half, :], kept_pair[whole_rows : whole_rows + half, :]
    gram[...] = dot_nt(high, kept_pair[half:whole_rows, :])
    gram[...] += dot_nt(low, kept_pair[half:whole_rows, :])
    gram[...] += dot_nt(high, kept_pair[whole_rows + half :, :])
    halves[0, half:, :] = gram[: half // 2, :]
    halves[1, half:, :] = gram[half // 2 :, :]
    copy = remote(halves.at[place.partner], crossed, cross_sem.at[0], cross_sem.at[1], {"gx": place.partner})
    copy.wait_recv()
    total[...] = halves[place.gx] + crossed[...]
    return copy


def kernel(
    plane, field, start_one, start_two, own_one, own_two, core, own, other, pair, pair_p, gram_pair, cross, crossed,
    gram, basis, partial, arrived, projected, kept, kept_pair, square, halves, crossed_two, core_parts, landed,
    load_sem, field_sem, cross_sem, pair_sem, trade_sem, core_sem, *sums
):
    place = Place(plane)
    gx, gy = place.gx, place.gy
    rows, cols, depth = field.shape
    place.greet()
    sums_one, sums_two = sums[: len(sums) // 2], sums[len(sums) // 2 :]
    sent = gram_one_sums(
        place, field, own, other, pair, pair_p, gram_pair, cross, crossed, load_sem, field_sem, cross_sem.at[0], sums_one[0]
    )
    sum_over_chips(place, *sums_one)
    unfold_sum(sums_one[3], gram)
    basis[...] = orthonormal(gram, start_one[...])
    pairs, trades, local = project(
        place, pair, basis, partial, arrived, projected, kept, pair_sem, trade_sem, cols, depth
    )
    own_one[...] = basis[pl.ds(pl.multiple_of(gx * rows, 8), rows), :]
    for copy in local:
        copy.wait()
    spread_kept(place, kept, kept_pair, gy, cols)
    for d in place.plane_order()[::-1]:
        for q in range(len(local)):
            trades[q, d].wait_recv()
        spread_kept(place, kept, kept_pair, place.plane_source(d), cols)
    sent.append(gram_two_sums(place, kept_pair, square, halves, crossed_two, cross_sem.at[1], sums_two[0]))
    sum_over_chips(place, *sums_two)
    unfold_sum(sums_two[3], gram)
    basis[...] = orthonormal(gram, start_two[...])
    own_two[...] = basis[pl.ds(pl.multiple_of(gy * cols, 8), cols), :]

    whole_rows, part_ranks, part_depth = kept.shape
    splits = depth // part_depth
    each = core.shape[1]
    basis_high, basis_low = split(basis[...].T)
    first = dot_nn(jnp.concatenate([basis_high, basis_low], axis=0), kept_pair[0:whole_rows, :])
    first = first[:RANK] + first[RANK:] + dot_nn(basis_high, kept_pair[whole_rows:, :])
    for r in range(part_ranks):
        core_parts[r] = first[:, r * part_depth : (r + 1) * part_depth]
    landing = landed.at[
        pl.ds(gy // splits * part_ranks, part_ranks),
        :,
        pl.ds(pl.multiple_of(gy % splits * part_depth, 128), part_depth),
    ]

    def piece(peer):
        return core_parts.at[:, pl.ds(pl.multiple_of(peer * each, 8), each), :]

    last = []
    for d in place.plane_order():
        peer = place.plane_peer(d)
        last.append(remote(piece(peer), landing, core_sem.at[0, d], core_sem.at[1, d], {"gy": peer}))
    stays = pltpu.make_async_copy(piece(gy), landing, core_sem.at[0, 0])
    stays.start()
    for copy in sent + pairs + list(trades.values()):
        copy.wait_send()
    stays.wait()
    for copy in last:
        copy.wait_recv()
    core[...] = landed[...]
    for copy in last:
        copy.wait_send()


PARTS = 4


def body(plane, field, start_one, start_two):
    rows, cols, depth = field.shape
    ny, nx, nz = plane
    planes = ny * nx
    splits = depth // 128
    part_ranks = RANK // 2 // (planes // splits)
    whole_rows = planes * cols
    half = whole_rows // 2
    dma = pltpu.SemaphoreType.DMA
    vmem = pl.BlockSpec(memory_space=pltpu.VMEM)
    core_shape = (RANK // 2, RANK // planes, depth)
    size = max(2 * rows, whole_rows)
    return pl.pallas_call(
        functools.partial(kernel, plane),
        out_shape=(
            jax.ShapeDtypeStruct((rows, RANK), f32),
            jax.ShapeDtypeStruct((cols, RANK), f32),
            jax.ShapeDtypeStruct(core_shape, f32),
        ),
        in_specs=[pl.BlockSpec(memory_space=pl.ANY), vmem, vmem],
        out_specs=(vmem, vmem, vmem),
        scratch_shapes=[
            pltpu.VMEM((cols, rows, depth), f32),
            pltpu.VMEM((cols // 2, rows, depth), f32),
            pltpu.VMEM((2 * rows, cols * depth), bf16),
            pltpu.VMEM((2 * rows, cols // 2 * depth), bf16),
            pltpu.VMEM((2 * rows, rows), f32),
            pltpu.VMEM((rows, rows), f32),
            pltpu.VMEM((rows // 2, rows), f32),
            pltpu.VMEM((size, size), f32),
            pltpu.VMEM((size, RANK), f32),
            pltpu.VMEM((cols, RANK, depth), f32),
            pltpu.VMEM((cols, RANK // 2, depth), f32),
            pltpu.VMEM((cols, RANK // 2, depth), f32),
            pltpu.VMEM((whole_rows, part_ranks, 128), f32),
            pltpu.VMEM((2 * whole_rows, part_ranks * 128), bf16),
            pltpu.VMEM((half, half), f32),
            pltpu.VMEM((2, half * 3 // 2, half), f32),
            pltpu.VMEM((half * 3 // 2, half), f32),
            pltpu.VMEM((part_ranks, RANK, 128), f32),
            pltpu.VMEM(core_shape, f32),
            dma((cols,)),
            dma((2, cols // 2)),
            dma((2, 2)),
            dma((2, PARTS)),
            dma((2, PARTS, planes)),
            dma((2, planes)),
            *sum_scratch(plane, rows * 3 // 2, rows),
            *sum_scratch(plane, half * 3 // 2, half),
        ],
        compiler_params=pltpu.CompilerParams(collective_id=0, has_side_effects=True, vmem_limit_bytes=VMEM_LIMIT),
        name="hosvd",
    )(field, start_one, start_two)


def solution(mesh):
    sizes = dict(mesh.shape)
    side = 4 if sizes["gy"] == 16 else 2
    plane = (sizes["gy"] // side, side, sizes["gz"])
    return jax.shard_map(
        functools.partial(body, plane),
        mesh=mesh,
        in_specs=(P("gx", "gy", "gz"), P(), P()),
        out_specs=(P("gx", None), P("gy", None), P("gx", "gy", "gz")),
        check_vma=False,
    )
```

```python
import functools

import jax
import jax.numpy as jnp
from jax import lax
from jax.experimental import pallas as pl
from jax.experimental.pallas import tpu as pltpu
from jax.sharding import PartitionSpec as P

RANK = 128
ITERS = 2
MESH = pl.DeviceIdType.MESH
f32 = jnp.float32
bf16 = jnp.bfloat16
highest = lax.Precision.HIGHEST
VMEM_LIMIT = 56 * 1024 * 1024


def split(value):
    high = value.astype(bf16)
    return high, (value - high.astype(f32)).astype(bf16)


def dot_nt(a, b, precision=None):
    return lax.dot_general(a, b, (((1,), (1,)), ((), ())), precision=precision, preferred_element_type=f32)


def dot_tn(a, b, precision=None):
    return lax.dot_general(a, b, (((0,), (0,)), ((), ())), precision=precision, preferred_element_type=f32)


def dot_nn(a, b, precision=None):
    return lax.dot_general(a, b, (((1,), (0,)), ((), ())), precision=precision, preferred_element_type=f32)


class Place:
    def __init__(self, plane):
        self.gx, self.gy, self.gz = (lax.axis_index(name) for name in ("gx", "gy", "gz"))
        self.partner = 1 - self.gx
        self.ny, self.nx, self.nz = plane
        self.np = self.ny * self.nx
        self.y, self.x = self.gy // self.nx, self.gy % self.nx

    def plane_peer(self, d):
        dy, dx = d // self.nx, d % self.nx
        return (self.y + dy) % self.ny * self.nx + (self.x + dx) % self.nx

    def plane_source(self, d):
        dy, dx = d // self.nx, d % self.nx
        return (self.y - dy) % self.ny * self.nx + (self.x - dx) % self.nx

    def plane_order(self):
        def hops(d):
            dy, dx = d // self.nx, d % self.nx
            return min(dy, self.ny - dy) + min(dx, self.nx - dx)

        return sorted(range(1, self.np), key=lambda d: (-hops(d), d))

    def z_peer(self, d):
        return (self.gz + d) % self.nz

    def others(self, kinds):
        found = []
        if "x" in kinds:
            found.append({"gx": self.partner})
        if "p" in kinds:
            found += [{"gy": self.plane_peer(d)} for d in range(1, self.np)]
        if "z" in kinds:
            found += [{"gz": self.z_peer(d)} for d in range(1, self.nz)]
        return found

    def greet(self):
        for peer in self.others("pzx"):
            pl.semaphore_signal(pltpu.get_barrier_semaphore(), inc=1, device_id=peer, device_id_type=MESH)

    def meet(self):
        pl.semaphore_wait(pltpu.get_barrier_semaphore(), len(self.others("pzx")))


def remote(src, dst, send_sem, recv_sem, device_id):
    copy = pltpu.make_async_remote_copy(
        src_ref=src, dst_ref=dst, send_sem=send_sem, recv_sem=recv_sem, device_id=device_id, device_id_type=MESH
    )
    copy.start()
    return copy


def sum_scratch(plane, rows, width):
    ny, nx, nz = plane
    planes = ny * nx
    chunk = rows // planes
    dma = pltpu.SemaphoreType.DMA
    return [
        pltpu.VMEM((rows, width), f32),
        pltpu.VMEM((planes, chunk, width), f32),
        pltpu.VMEM((nz, chunk, width), f32),
        pltpu.VMEM((2, rows, width), f32),
        dma((2, planes)),
        dma((2, nz)),
        dma((2, planes)),
        dma((2,)),
    ]


def sum_over_chips(place, total, parts, zparts, whole, rs_sem, z_sem, ag_sem, x_sem):
    chunk = total.shape[0] // place.np
    order = place.plane_order()
    sent = []
    for d in order:
        peer = place.plane_peer(d)
        piece = total.at[pl.ds(pl.multiple_of(peer * chunk, 8), chunk), :]
        sent.append(remote(piece, parts.at[d], rs_sem.at[0, d], rs_sem.at[1, d], {"gy": peer}))
    own = pl.ds(pl.multiple_of(place.gy * chunk, 8), chunk)
    value = total[own, :]
    for d, copy in list(zip(order, sent))[::-1]:
        copy.wait_recv()
        value = value + parts[d]
    zparts[place.gz] = value
    mine = zparts.at[place.gz]
    copies = [
        remote(mine, mine, z_sem.at[0, d], z_sem.at[1, d], {"gz": place.z_peer(d)})
        for d in sorted(range(1, place.nz), key=lambda d: -min(d, place.nz - d))
    ]
    for copy in copies:
        copy.wait_recv()
    value = zparts[0]
    for z in range(1, place.nz):
        value = value + zparts[z]
    whole[place.gx, own, :] = value
    sent += copies
    block = whole.at[place.gx, own, :]
    copies = [remote(block, block, ag_sem.at[0, d], ag_sem.at[1, d], {"gy": place.plane_peer(d)}) for d in order]
    for copy in copies:
        copy.wait_recv()
    mine = whole.at[place.gx]
    last = remote(mine, mine, x_sem.at[0], x_sem.at[1], {"gx": place.partner})
    for copy in sent + copies:
        copy.wait_send()
    last.wait()


def unfold_sum(whole, terms):
    half = whole.shape[2]
    upper = jnp.concatenate([whole[0, half:, :], whole[1, half:, :]], axis=0)
    first, second = slice(0, half), slice(half, 2 * half)
    blocks = {
        (first, first): whole[0, 0:half, :],
        (second, second): whole[1, 0:half, :],
        (first, second): upper,
        (second, first): upper.T,
    }
    for (rows, cols), block in blocks.items():
        terms[0, rows, cols], terms[1, rows, cols], terms[2, rows, cols] = split3(block)


def small_inverse_factor(entry):
    n = len(entry)
    entry = [list(row) for row in entry]
    below = [[None] * n for _ in range(n)]
    result = [[None] * (i + 1) for i in range(n)]
    for k in range(0, n, 2):
        a, b, c = entry[k][k], entry[k + 1][k], entry[k + 1][k + 1]
        det = a * c - b * b
        inverse = reciprocal(det)
        over = 1.0 / a
        ratio = b * over
        scale_one, scale_two = lax.rsqrt(a), lax.rsqrt(det * over)
        for j in range(k):
            result[k][j] = below[k][j] * scale_one
            result[k + 1][j] = (below[k + 1][j] - ratio * below[k][j]) * scale_two
        result[k][k] = scale_one
        result[k + 1][k] = -ratio * scale_two
        result[k + 1][k + 1] = scale_two
        factors = {}
        for i in range(k + 2, n):
            p, q = entry[i][k], entry[i][k + 1]
            factors[i] = (c * p - b * q) * inverse, (a * q - b * p) * inverse
        for i in range(k + 2, n):
            f, g = factors[i]
            for j in range(k + 2, i + 1):
                entry[i][j] = entry[i][j] - (f * entry[j][k] + g * entry[j][k + 1])
            for j in range(k):
                below[i][j] = below[i][j] - (f * below[k][j] + g * below[k + 1][j])
            below[i][k], below[i][k + 1] = -f, -g
    return result


def reciprocal(value):
    return 1.0 / value


def tree(terms):
    while len(terms) > 1:
        terms = [a + b for a, b in zip(terms[::2], terms[1::2])] + ([terms[-1]] if len(terms) % 2 else [])
    return terms[0]


def inverse_factor(crossed, held):
    n = crossed.shape[0]
    sub = lax.broadcasted_iota(jnp.int32, (8, n), 0)
    lane = lax.broadcasted_iota(jnp.int32, (8, n), 1)
    tiles = [crossed[8 * t : 8 * t + 8, :] for t in range(n // 8)]
    found = []

    def lanes_of(tile, k):
        return jnp.broadcast_to(tile[:, k : k + 1], (8, n))

    def row_of(t, which, k):
        return jnp.broadcast_to(held[t, which, k : k + 1, :], (8, n))

    for t in range(n // 8):
        first = 8 * t
        inside = (lane >= first) & (lane < first + 8)
        for k in range(8):
            held[t, k] = lanes_of(tiles[t], first + k)
        held[t, 8] = jnp.where(inside, jnp.where(lane == sub + first, 1.0, 0.0), tiles[t])
        factor = small_inverse_factor([[row_of(t, j, i) for j in range(i + 1)] for i in range(8)])
        spread = [row_of(t, 8, k) for k in range(8)]
        rows = [tree([factor[i][j] * spread[j] for j in range(i + 1)]) for i in range(8)]
        value = rows[0]
        for i in range(1, 8):
            value = jnp.where(sub == i, rows[i], value)
        found.append(jnp.where(lane < first + 8, value, 0.0))
        if t + 1 == n // 8:
            break
        solved = [tree([factor[i][k] * rows[i] for i in range(k, 8)]) for k in range(8)]
        for u in range(t + 1, n // 8):
            terms = [lanes_of(tiles[u], first + k) * solved[k] for k in range(8)]
            tiles[u] = jnp.where(inside, 0.0, tiles[u]) - tree(terms)
    return jnp.concatenate(found, axis=0)


def split3(value):
    high = value.astype(bf16)
    rest = value - high.astype(f32)
    middle = rest.astype(bf16)
    return high, middle, (rest - middle.astype(f32)).astype(bf16)


def times(left, right):
    n = left.shape[0]
    high, middle, low = split3(left)
    one = dot_nn(jnp.concatenate([high, middle, low], axis=0), right[0])
    two = dot_nn(jnp.concatenate([high, middle], axis=0), right[1])
    three = dot_nn(high, right[2])
    return one[:n] + (one[n : 2 * n] + two[:n]) + (one[2 * n :] + two[n:] + three)


def square(rows):
    n = rows.shape[0]
    high, middle, low = split3(rows)
    one = dot_nt(jnp.concatenate([high, middle, low], axis=0), high)
    mid, last = one[n : 2 * n], one[2 * n :]
    return one[:n] + (mid + mid.T) + (last + last.T + dot_nt(middle, middle))


def orthonormal(terms, start, held):
    assert ITERS == 2
    product = times(start, terms)
    inverse = inverse_factor(square(product), held)
    second = times(product, terms)
    product = times(inverse, split3(second))
    return times(inverse_factor(square(product), held), split3(product))


def split_block(block, at, pair):
    rows = block.shape[0]
    pair[0:rows, at], pair[rows:, at] = split(block)


def gram_one_sums(place, field, own, other, pair, pair_p, gram, cross, crossed, load_sem, field_sem, cross_sem, total):
    rows, cols, depth = field.shape
    half = cols // 2
    gx, partner = place.gx, place.partner
    step = 8 * depth
    loads = []
    for j in range(cols):
        loads.append(pltpu.make_async_copy(field.at[:, j, :], own.at[j], load_sem.at[j]))
        loads[-1].start()
    gram[...] = jnp.zeros_like(gram)
    sends = []
    for c in range(cols // 8):
        for j in range(8 * c, 8 * c + 8):
            loads[j].wait()
            split_block(own[j], slice(j * depth, (j + 1) * depth), pair)
        at = slice(c * step, (c + 1) * step)
        gram[...] += dot_nt(pair[:, at], pair[0:rows, at])
        if c == 0:
            place.meet()
            for j in range(half):
                sends.append(
                    remote(
                        field.at[:, partner * half + j, :],
                        other.at[j],
                        field_sem.at[0, j],
                        field_sem.at[1, j],
                        {"gx": partner},
                    )
                )
    cross[...] = jnp.zeros_like(cross)
    for c in range(half // 8):
        for j in range(8 * c, 8 * c + 8):
            sends[j].wait_recv()
            split_block(other[j], slice(j * depth, (j + 1) * depth), pair_p)
        at = slice(c * step, (c + 1) * step)
        mine = pl.ds(pl.multiple_of(gx * half * depth + c * step, step), step)
        both = dot_nt(pair[:, mine], pair_p[0:rows, at])
        cross[...] += both[0:rows] + both[rows:] + dot_nt(pair[0:rows, mine], pair_p[rows:, at])
    value = cross[...]
    cross[...] = jnp.where(gx == 0, value, value.T)
    quarter = rows // 2
    copy = remote(
        cross.at[pl.ds(pl.multiple_of(partner * quarter, 8), quarter), :],
        crossed,
        cross_sem.at[0],
        cross_sem.at[1],
        {"gx": partner},
    )
    total[0:rows, :] = gram[0:rows, :] + gram[rows:, :] + gram[rows:, :].T
    copy.wait_recv()
    total[rows:, :] = cross[pl.ds(pl.multiple_of(gx * quarter, 8), quarter), :] + crossed[...]
    return sends + [copy]


def project(place, pair, basis, partial, arrived, projected, kept, pair_sem, trade_sem, cols, depth):
    gx, gy, partner = place.gx, place.gy, place.partner
    rows = pair.shape[0] // 2
    ranks = RANK // 2
    parts = trade_sem.shape[1]
    each = cols // parts
    _, part_ranks, part_depth = kept.shape
    splits = depth // part_depth
    basis_high, basis_low = split(basis[:, pl.ds(pl.multiple_of(gx * rows, 128), rows)])
    both = jnp.concatenate([basis_high, basis_low], axis=0)
    here = pl.ds(pl.multiple_of(gx * ranks, 8), ranks)
    there = pl.ds(pl.multiple_of(partner * ranks, 8), ranks)

    def piece(q, peer):
        return projected.at[
            each * q : each * (q + 1),
            pl.ds(pl.multiple_of(peer // splits * part_ranks, 8), part_ranks),
            pl.ds(pl.multiple_of(peer % splits * part_depth, 128), part_depth),
        ]

    def landing(q):
        return kept.at[pl.ds(gy * cols + each * q, each), :, :]

    def partials(q):
        for j in range(each * q, each * (q + 1)):
            at = slice(j * depth, (j + 1) * depth)
            first = dot_nn(both, pair[0:rows, at])
            partial[j] = first[:RANK] + first[RANK:] + dot_nn(basis_high, pair[rows:, at])
        at = slice(each * q, each * (q + 1))
        return remote(partial.at[at, there, :], arrived.at[at], pair_sem.at[0, q], pair_sem.at[1, q], {"gx": partner})

    order = place.plane_order()
    pairs, trades = [partials(0)], {}
    for q in range(parts):
        if q + 1 < parts:
            pairs.append(partials(q + 1))
        pairs[q].wait_recv()
        for j in range(each * q, each * (q + 1)):
            projected[j] = partial[j, here, :] + arrived[j]
        for d in order:
            peer = place.plane_peer(d)
            trades[q, d] = remote(
                piece(q, peer), landing(q), trade_sem.at[0, q, d], trade_sem.at[1, q, d], {"gy": peer}
            )
    local = []
    for q in range(parts):
        local.append(pltpu.make_async_copy(piece(q, gy), landing(q), trade_sem.at[0, q, 0]))
        local[-1].start()
    return pairs, trades, local


def spread_kept(place, kept, kept_pair, peer, cols):
    whole_rows, part_ranks, lanes = kept.shape
    flat = kept.reshape(whole_rows * part_ranks, lanes)
    for r in range(part_ranks):
        value = flat[pl.ds(peer * cols * part_ranks + r, cols, stride=part_ranks), :]
        at = slice(r * lanes, (r + 1) * lanes)
        first = pl.ds(pl.multiple_of(peer * cols, 16), cols)
        second = pl.ds(pl.multiple_of(whole_rows + peer * cols, 16), cols)
        kept_pair[first, at], kept_pair[second, at] = split(value)


def gram_two_sums(place, kept_pair, gram, halves, crossed, cross_sem, total):
    whole_rows = kept_pair.shape[0] // 2
    half = whole_rows // 2
    for k in range(2):
        high = kept_pair[half * k : half * (k + 1), :]
        low = kept_pair[whole_rows + half * k : whole_rows + half * (k + 1), :]
        gram[...] = dot_nt(low, high)
        halves[k, 0:half, :] = dot_nt(high, high)
        halves[k, 0:half, :] += gram[...] + gram[...].T
    high, low = kept_pair[0:half, :], kept_pair[whole_rows : whole_rows + half, :]
    gram[...] = dot_nt(high, kept_pair[half:whole_rows, :])
    gram[...] += dot_nt(low, kept_pair[half:whole_rows, :])
    gram[...] += dot_nt(high, kept_pair[whole_rows + half :, :])
    halves[0, half:, :] = gram[: half // 2, :]
    halves[1, half:, :] = gram[half // 2 :, :]
    copy = remote(halves.at[place.partner], crossed, cross_sem.at[0], cross_sem.at[1], {"gx": place.partner})
    copy.wait_recv()
    total[...] = halves[place.gx] + crossed[...]
    return copy


def kernel(
    plane, field, start_one, start_two, own_one, own_two, core, own, other, pair, pair_p, gram_pair, cross, crossed,
    terms, basis, start, turned, held, partial, arrived, projected, kept, kept_pair, square, halves, crossed_two, core_parts, landed,
    load_sem, field_sem, cross_sem, pair_sem, trade_sem, core_sem, *sums
):
    place = Place(plane)
    gx, gy = place.gx, place.gy
    rows, cols, depth = field.shape
    place.greet()
    start[0] = start_one[...].T
    start[1] = start_two[...].T
    sums_one, sums_two = sums[: len(sums) // 2], sums[len(sums) // 2 :]
    sent = gram_one_sums(
        place, field, own, other, pair, pair_p, gram_pair, cross, crossed, load_sem, field_sem, cross_sem.at[0], sums_one[0]
    )
    sum_over_chips(place, *sums_one)
    unfold_sum(sums_one[3], terms)
    basis[...] = orthonormal(terms, start[0], held)
    pairs, trades, local = project(
        place, pair, basis, partial, arrived, projected, kept, pair_sem, trade_sem, cols, depth
    )
    own_one[...] = basis[:, pl.ds(pl.multiple_of(gx * rows, 128), rows)].T
    for copy in local:
        copy.wait()
    spread_kept(place, kept, kept_pair, gy, cols)
    for d in place.plane_order()[::-1]:
        for q in range(len(local)):
            trades[q, d].wait_recv()
        spread_kept(place, kept, kept_pair, place.plane_source(d), cols)
    sent.append(gram_two_sums(place, kept_pair, square, halves, crossed_two, cross_sem.at[1], sums_two[0]))
    sum_over_chips(place, *sums_two)
    unfold_sum(sums_two[3], terms)
    basis[...] = orthonormal(terms, start[1], held)
    whole_rows, part_ranks, part_depth = kept.shape
    splits = depth // part_depth
    each = core.shape[1]
    basis_high, basis_low = split(basis[...])
    first = dot_nn(jnp.concatenate([basis_high, basis_low], axis=0), kept_pair[0:whole_rows, :])
    first = first[:RANK] + first[RANK:] + dot_nn(basis_high, kept_pair[whole_rows:, :])
    for r in range(part_ranks):
        core_parts[r] = first[:, r * part_depth : (r + 1) * part_depth]
    landing = landed.at[
        pl.ds(gy // splits * part_ranks, part_ranks),
        :,
        pl.ds(pl.multiple_of(gy % splits * part_depth, 128), part_depth),
    ]

    def piece(peer):
        return core_parts.at[:, pl.ds(pl.multiple_of(peer * each, 8), each), :]

    last = []
    for d in place.plane_order():
        peer = place.plane_peer(d)
        last.append(remote(piece(peer), landing, core_sem.at[0, d], core_sem.at[1, d], {"gy": peer}))
    stays = pltpu.make_async_copy(piece(gy), landing, core_sem.at[0, 0])
    stays.start()
    turned[...] = basis[...].T
    own_two[...] = turned[pl.ds(pl.multiple_of(gy * cols, 8), cols), :]
    for copy in sent + pairs + list(trades.values()):
        copy.wait_send()
    stays.wait()
    for copy in last:
        copy.wait_recv()
    core[...] = landed[...]
    for copy in last:
        copy.wait_send()


def deliver(*refs):
    count = len(refs) // 2
    sem = refs[-1]
    copies = [pltpu.make_async_copy(refs[k], refs[count + k], sem.at[k]) for k in range(count)]
    for copy in copies:
        copy.start()
    for copy in copies:
        copy.wait()


PARTS = 4


def body(plane, field, start_one, start_two):
    rows, cols, depth = field.shape
    ny, nx, nz = plane
    planes = ny * nx
    splits = depth // 128
    part_ranks = RANK // 2 // (planes // splits)
    whole_rows = planes * cols
    half = whole_rows // 2
    dma = pltpu.SemaphoreType.DMA
    vmem = pl.BlockSpec(memory_space=pltpu.VMEM)
    core_shape = (RANK // 2, RANK // planes, depth)
    size = max(2 * rows, whole_rows)
    outs = pl.pallas_call(
        functools.partial(kernel, plane),
        out_shape=(
            jax.ShapeDtypeStruct((rows, RANK), f32),
            jax.ShapeDtypeStruct((cols, RANK), f32),
            jax.ShapeDtypeStruct(core_shape, f32),
        ),
        in_specs=[pl.BlockSpec(memory_space=pl.ANY), vmem, vmem],
        out_specs=(vmem, vmem, vmem),
        scratch_shapes=[
            pltpu.VMEM((cols, rows, depth), f32),
            pltpu.VMEM((cols // 2, rows, depth), f32),
            pltpu.VMEM((2 * rows, cols * depth), bf16),
            pltpu.VMEM((2 * rows, cols // 2 * depth), bf16),
            pltpu.VMEM((2 * rows, rows), f32),
            pltpu.VMEM((rows, rows), f32),
            pltpu.VMEM((rows // 2, rows), f32),
            pltpu.VMEM((3, size, size), bf16),
            pltpu.VMEM((RANK, size), f32),
            pltpu.VMEM((2, RANK, size), f32),
            pltpu.VMEM((size, RANK), f32),
            pltpu.VMEM((RANK // 8, 9, 8, RANK), f32),
            pltpu.VMEM((cols, RANK, depth), f32),
            pltpu.VMEM((cols, RANK // 2, depth), f32),
            pltpu.VMEM((cols, RANK // 2, depth), f32),
            pltpu.VMEM((whole_rows, part_ranks, 128), f32),
            pltpu.VMEM((2 * whole_rows, part_ranks * 128), bf16),
            pltpu.VMEM((half, half), f32),
            pltpu.VMEM((2, half * 3 // 2, half), f32),
            pltpu.VMEM((half * 3 // 2, half), f32),
            pltpu.VMEM((part_ranks, RANK, 128), f32),
            pltpu.VMEM(core_shape, f32),
            dma((cols,)),
            dma((2, cols // 2)),
            dma((2, 2)),
            dma((2, PARTS)),
            dma((2, PARTS, planes)),
            dma((2, planes)),
            *sum_scratch(plane, rows * 3 // 2, rows),
            *sum_scratch(plane, half * 3 // 2, half),
        ],
        compiler_params=pltpu.CompilerParams(collective_id=0, has_side_effects=True, vmem_limit_bytes=VMEM_LIMIT),
        name="hosvd",
    )(field, start_one, start_two)
    anywhere = pl.BlockSpec(memory_space=pl.ANY)
    return pl.pallas_call(
        deliver,
        out_shape=tuple(jax.ShapeDtypeStruct(out.shape, f32) for out in outs),
        in_specs=[anywhere] * len(outs),
        out_specs=(anywhere,) * len(outs),
        scratch_shapes=[dma((len(outs),))],
        name="deliver",
    )(*outs)


def solution(mesh):
    sizes = dict(mesh.shape)
    side = 4 if sizes["gy"] == 16 else 2
    plane = (sizes["gy"] // side, side, sizes["gz"])
    return jax.shard_map(
        functools.partial(body, plane),
        mesh=mesh,
        in_specs=(P("gx", "gy", "gz"), P(), P()),
        out_specs=(P("gx", None), P("gy", None), P("gx", "gy", "gz")),
        check_vma=False,
    )
```

```python
import functools

import jax
import jax.numpy as jnp
from jax import lax
from jax.experimental import pallas as pl
from jax.experimental.pallas import tpu as pltpu
from jax.sharding import PartitionSpec as P

RANK = 128
ITERS = 2
MESH = pl.DeviceIdType.MESH
f32 = jnp.float32
bf16 = jnp.bfloat16
highest = lax.Precision.HIGHEST
VMEM_LIMIT = 56 * 1024 * 1024


def split(value):
    high = value.astype(bf16)
    return high, (value - high.astype(f32)).astype(bf16)


def dot_nt(a, b, precision=None):
    return lax.dot_general(a, b, (((1,), (1,)), ((), ())), precision=precision, preferred_element_type=f32)


def dot_tn(a, b, precision=None):
    return lax.dot_general(a, b, (((0,), (0,)), ((), ())), precision=precision, preferred_element_type=f32)


def dot_nn(a, b, precision=None):
    return lax.dot_general(a, b, (((1,), (0,)), ((), ())), precision=precision, preferred_element_type=f32)


class Place:
    def __init__(self, plane):
        self.gx, self.gy, self.gz = (lax.axis_index(name) for name in ("gx", "gy", "gz"))
        self.partner = 1 - self.gx
        self.ny, self.nx, self.nz = plane
        self.np = self.ny * self.nx
        self.y, self.x = self.gy // self.nx, self.gy % self.nx

    def plane_peer(self, d):
        dy, dx = d // self.nx, d % self.nx
        return (self.y + dy) % self.ny * self.nx + (self.x + dx) % self.nx

    def plane_source(self, d):
        dy, dx = d // self.nx, d % self.nx
        return (self.y - dy) % self.ny * self.nx + (self.x - dx) % self.nx

    def plane_order(self):
        def hops(d):
            dy, dx = d // self.nx, d % self.nx
            return min(dy, self.ny - dy) + min(dx, self.nx - dx)

        return sorted(range(1, self.np), key=lambda d: (-hops(d), d))

    def z_peer(self, d):
        return (self.gz + d) % self.nz

    def others(self, kinds):
        found = []
        if "x" in kinds:
            found.append({"gx": self.partner})
        if "p" in kinds:
            found += [{"gy": self.plane_peer(d)} for d in range(1, self.np)]
        if "z" in kinds:
            found += [{"gz": self.z_peer(d)} for d in range(1, self.nz)]
        return found

    def greet(self):
        for peer in self.others("pzx"):
            pl.semaphore_signal(pltpu.get_barrier_semaphore(), inc=1, device_id=peer, device_id_type=MESH)

    def meet(self):
        pl.semaphore_wait(pltpu.get_barrier_semaphore(), len(self.others("pzx")))


def remote(src, dst, send_sem, recv_sem, device_id):
    copy = pltpu.make_async_remote_copy(
        src_ref=src, dst_ref=dst, send_sem=send_sem, recv_sem=recv_sem, device_id=device_id, device_id_type=MESH
    )
    copy.start()
    return copy


def sum_scratch(plane, rows, width):
    ny, nx, nz = plane
    planes = ny * nx
    chunk = rows // planes
    dma = pltpu.SemaphoreType.DMA
    return [
        pltpu.VMEM((rows, width), f32),
        pltpu.VMEM((planes, chunk, width), f32),
        pltpu.VMEM((nz, chunk, width), f32),
        pltpu.VMEM((2, rows, width), f32),
        dma((2, planes)),
        dma((2, nz)),
        dma((2, planes)),
        dma((2,)),
    ]


def sum_over_chips(place, total, parts, zparts, whole, rs_sem, z_sem, ag_sem, x_sem):
    chunk = total.shape[0] // place.np
    order = place.plane_order()
    sent = []
    for d in order:
        peer = place.plane_peer(d)
        piece = total.at[pl.ds(pl.multiple_of(peer * chunk, 8), chunk), :]
        sent.append(remote(piece, parts.at[d], rs_sem.at[0, d], rs_sem.at[1, d], {"gy": peer}))
    own = pl.ds(pl.multiple_of(place.gy * chunk, 8), chunk)
    value = total[own, :]
    for d, copy in list(zip(order, sent))[::-1]:
        copy.wait_recv()
        value = value + parts[d]
    zparts[place.gz] = value
    mine = zparts.at[place.gz]
    copies = [
        remote(mine, mine, z_sem.at[0, d], z_sem.at[1, d], {"gz": place.z_peer(d)})
        for d in sorted(range(1, place.nz), key=lambda d: -min(d, place.nz - d))
    ]
    for copy in copies:
        copy.wait_recv()
    value = zparts[0]
    for z in range(1, place.nz):
        value = value + zparts[z]
    whole[place.gx, own, :] = value
    sent += copies
    block = whole.at[place.gx, own, :]
    copies = [remote(block, block, ag_sem.at[0, d], ag_sem.at[1, d], {"gy": place.plane_peer(d)}) for d in order]
    for copy in copies:
        copy.wait_recv()
    mine = whole.at[place.gx]
    last = remote(mine, mine, x_sem.at[0], x_sem.at[1], {"gx": place.partner})
    for copy in sent + copies:
        copy.wait_send()
    last.wait()


def unfold_sum(whole, terms):
    half = whole.shape[2]
    upper = jnp.concatenate([whole[0, half:, :], whole[1, half:, :]], axis=0)
    first, second = slice(0, half), slice(half, 2 * half)
    blocks = {
        (first, first): whole[0, 0:half, :],
        (second, second): whole[1, 0:half, :],
        (first, second): upper,
        (second, first): upper.T,
    }
    for (rows, cols), block in blocks.items():
        terms[0, rows, cols], terms[1, rows, cols], terms[2, rows, cols] = split3(block)


def small_inverse_factor(entry):
    n = len(entry)
    entry = [list(row) for row in entry]
    below = [[None] * n for _ in range(n)]
    result = [[None] * (i + 1) for i in range(n)]
    for k in range(0, n, 2):
        a, b, c = entry[k][k], entry[k + 1][k], entry[k + 1][k + 1]
        det = a * c - b * b
        inverse = reciprocal(det)
        over = 1.0 / a
        ratio = b * over
        scale_one, scale_two = lax.rsqrt(a), lax.rsqrt(det * over)
        for j in range(k):
            result[k][j] = below[k][j] * scale_one
            result[k + 1][j] = (below[k + 1][j] - ratio * below[k][j]) * scale_two
        result[k][k] = scale_one
        result[k + 1][k] = -ratio * scale_two
        result[k + 1][k + 1] = scale_two
        factors = {}
        for i in range(k + 2, n):
            p, q = entry[i][k], entry[i][k + 1]
            factors[i] = (c * p - b * q) * inverse, (a * q - b * p) * inverse
        for i in range(k + 2, n):
            f, g = factors[i]
            for j in range(k + 2, i + 1):
                entry[i][j] = entry[i][j] - (f * entry[j][k] + g * entry[j][k + 1])
            for j in range(k):
                below[i][j] = below[i][j] - (f * below[k][j] + g * below[k + 1][j])
            below[i][k], below[i][k + 1] = -f, -g
    return result


def reciprocal(value):
    return 1.0 / value


def tree(terms):
    while len(terms) > 1:
        terms = [a + b for a, b in zip(terms[::2], terms[1::2])] + ([terms[-1]] if len(terms) % 2 else [])
    return terms[0]


def inverse_factor(crossed, held):
    n = crossed.shape[0]
    sub = lax.broadcasted_iota(jnp.int32, (8, n), 0)
    lane = lax.broadcasted_iota(jnp.int32, (8, n), 1)
    tiles = [crossed[8 * t : 8 * t + 8, :] for t in range(n // 8)]
    found = []

    def lanes_of(tile, k):
        return jnp.broadcast_to(tile[:, k : k + 1], (8, n))

    def row_of(t, which, k):
        return jnp.broadcast_to(held[t, which, k : k + 1, :], (8, n))

    for t in range(n // 8):
        first = 8 * t
        inside = (lane >= first) & (lane < first + 8)
        for k in range(8):
            held[t, k] = lanes_of(tiles[t], first + k)
        held[t, 8] = jnp.where(inside, jnp.where(lane == sub + first, 1.0, 0.0), tiles[t])
        factor = small_inverse_factor([[row_of(t, j, i) for j in range(i + 1)] for i in range(8)])
        spread = [row_of(t, 8, k) for k in range(8)]
        rows = [tree([factor[i][j] * spread[j] for j in range(i + 1)]) for i in range(8)]
        value = rows[0]
        for i in range(1, 8):
            value = jnp.where(sub == i, rows[i], value)
        found.append(jnp.where(lane < first + 8, value, 0.0))
        if t + 1 == n // 8:
            break
        solved = [tree([factor[i][k] * rows[i] for i in range(k, 8)]) for k in range(8)]
        for u in range(t + 1, n // 8):
            terms = [lanes_of(tiles[u], first + k) * solved[k] for k in range(8)]
            tiles[u] = jnp.where(inside, 0.0, tiles[u]) - tree(terms)
    return jnp.concatenate(found, axis=0)


def split3(value):
    high = value.astype(bf16)
    rest = value - high.astype(f32)
    middle = rest.astype(bf16)
    return high, middle, (rest - middle.astype(f32)).astype(bf16)


def times(left, right):
    n = left.shape[0]
    high, middle, low = split3(left)
    one = dot_nn(jnp.concatenate([high, middle, low], axis=0), right[0])
    two = dot_nn(jnp.concatenate([high, middle], axis=0), right[1])
    three = dot_nn(high, right[2])
    return one[:n] + (one[n : 2 * n] + two[:n]) + (one[2 * n :] + two[n:] + three)


def square(rows):
    n = rows.shape[0]
    high, middle, low = split3(rows)
    one = dot_nt(jnp.concatenate([high, middle, low], axis=0), high)
    mid, last = one[n : 2 * n], one[2 * n :]
    return one[:n] + (mid + mid.T) + (last + last.T + dot_nt(middle, middle))


def orthonormal(terms, start, held):
    assert ITERS == 2
    product = times(start, terms)
    inverse = inverse_factor(square(product), held)
    second = times(product, terms)
    product = times(inverse, split3(second))
    return times(inverse_factor(square(product), held), split3(product))


def split_block(block, at, pair):
    rows = block.shape[0]
    pair[0:rows, at], pair[rows:, at] = split(block)


def gram_one_sums(place, field, own, other, pair, pair_p, gram, cross, crossed, load_sem, field_sem, cross_sem, total):
    rows, cols, depth = field.shape
    half = cols // 2
    gx, partner = place.gx, place.partner
    step = 8 * depth
    loads = []
    for j in range(cols):
        loads.append(pltpu.make_async_copy(field.at[:, j, :], own.at[j], load_sem.at[j]))
        loads[-1].start()
    gram[...] = jnp.zeros_like(gram)
    sends = []
    for c in range(cols // 8):
        for j in range(8 * c, 8 * c + 8):
            loads[j].wait()
            split_block(own[j], slice(j * depth, (j + 1) * depth), pair)
        at = slice(c * step, (c + 1) * step)
        gram[...] += dot_nt(pair[:, at], pair[0:rows, at])
        if c == 0:
            place.meet()
            for j in range(half):
                sends.append(
                    remote(
                        field.at[:, partner * half + j, :],
                        other.at[j],
                        field_sem.at[0, j],
                        field_sem.at[1, j],
                        {"gx": partner},
                    )
                )
    cross[...] = jnp.zeros_like(cross)
    for c in range(half // 8):
        for j in range(8 * c, 8 * c + 8):
            sends[j].wait_recv()
            split_block(other[j], slice(j * depth, (j + 1) * depth), pair_p)
        at = slice(c * step, (c + 1) * step)
        mine = pl.ds(pl.multiple_of(gx * half * depth + c * step, step), step)
        both = dot_nt(pair[:, mine], pair_p[0:rows, at])
        cross[...] += both[0:rows] + both[rows:] + dot_nt(pair[0:rows, mine], pair_p[rows:, at])
    value = cross[...]
    cross[...] = jnp.where(gx == 0, value, value.T)
    quarter = rows // 2
    copy = remote(
        cross.at[pl.ds(pl.multiple_of(partner * quarter, 8), quarter), :],
        crossed,
        cross_sem.at[0],
        cross_sem.at[1],
        {"gx": partner},
    )
    total[0:rows, :] = gram[0:rows, :] + gram[rows:, :] + gram[rows:, :].T
    copy.wait_recv()
    total[rows:, :] = cross[pl.ds(pl.multiple_of(gx * quarter, 8), quarter), :] + crossed[...]
    return sends + [copy]


def project(place, pair, basis, partial, arrived, projected, kept, pair_sem, trade_sem, cols, depth):
    gx, gy, partner = place.gx, place.gy, place.partner
    rows = pair.shape[0] // 2
    ranks = RANK // 2
    sizes = parts_of(cols)
    spans = [slice(sum(sizes[:q]), sum(sizes[: q + 1])) for q in range(len(sizes))]
    _, part_ranks, part_depth = kept.shape
    splits = depth // part_depth
    basis_high, basis_low = split(basis[:, pl.ds(pl.multiple_of(gx * rows, 128), rows)])
    both = jnp.concatenate([basis_high, basis_low], axis=0)
    here = pl.ds(pl.multiple_of(gx * ranks, 8), ranks)
    there = pl.ds(pl.multiple_of(partner * ranks, 8), ranks)

    def piece(q, peer):
        return projected.at[
            spans[q],
            pl.ds(pl.multiple_of(peer // splits * part_ranks, 8), part_ranks),
            pl.ds(pl.multiple_of(peer % splits * part_depth, 128), part_depth),
        ]

    def landing(q):
        return kept.at[pl.ds(gy * cols + spans[q].start, sizes[q]), :, :]

    def partials(q):
        for j in range(spans[q].start, spans[q].stop):
            at = slice(j * depth, (j + 1) * depth)
            first = dot_nn(both, pair[0:rows, at])
            partial[j] = first[:RANK] + first[RANK:] + dot_nn(basis_high, pair[rows:, at])
        at = spans[q]
        return remote(partial.at[at, there, :], arrived.at[at], pair_sem.at[0, q], pair_sem.at[1, q], {"gx": partner})

    order = place.plane_order()
    pairs, trades = [partials(0)], {}
    for q in range(len(sizes)):
        if q + 1 < len(sizes):
            pairs.append(partials(q + 1))
        pairs[q].wait_recv()
        for j in range(spans[q].start, spans[q].stop):
            projected[j] = partial[j, here, :] + arrived[j]
        for d in order:
            peer = place.plane_peer(d)
            trades[q, d] = remote(
                piece(q, peer), landing(q), trade_sem.at[0, q, d], trade_sem.at[1, q, d], {"gy": peer}
            )
    local = []
    for q in range(len(sizes)):
        local.append(pltpu.make_async_copy(piece(q, gy), landing(q), trade_sem.at[0, q, 0]))
        local[-1].start()
    return pairs, trades, local


def spread_kept(place, kept, kept_pair, peer, cols):
    whole_rows, part_ranks, lanes = kept.shape
    flat = kept.reshape(whole_rows * part_ranks, lanes)
    for r in range(part_ranks):
        value = flat[pl.ds(peer * cols * part_ranks + r, cols, stride=part_ranks), :]
        at = slice(r * lanes, (r + 1) * lanes)
        first = pl.ds(pl.multiple_of(peer * cols, 16), cols)
        second = pl.ds(pl.multiple_of(whole_rows + peer * cols, 16), cols)
        kept_pair[first, at], kept_pair[second, at] = split(value)


def gram_two_sums(place, kept_pair, gram, halves, crossed, cross_sem, total):
    whole_rows = kept_pair.shape[0] // 2
    half = whole_rows // 2
    for k in range(2):
        high = kept_pair[half * k : half * (k + 1), :]
        low = kept_pair[whole_rows + half * k : whole_rows + half * (k + 1), :]
        gram[...] = dot_nt(low, high)
        halves[k, 0:half, :] = dot_nt(high, high)
        halves[k, 0:half, :] += gram[...] + gram[...].T
    high, low = kept_pair[0:half, :], kept_pair[whole_rows : whole_rows + half, :]
    gram[...] = dot_nt(high, kept_pair[half:whole_rows, :])
    gram[...] += dot_nt(low, kept_pair[half:whole_rows, :])
    gram[...] += dot_nt(high, kept_pair[whole_rows + half :, :])
    halves[0, half:, :] = gram[: half // 2, :]
    halves[1, half:, :] = gram[half // 2 :, :]
    copy = remote(halves.at[place.partner], crossed, cross_sem.at[0], cross_sem.at[1], {"gx": place.partner})
    copy.wait_recv()
    total[...] = halves[place.gx] + crossed[...]
    return copy


def kernel(
    plane, field, start_one, start_two, own_one, own_two, core, own, other, pair, pair_p, gram_pair, cross, crossed,
    terms, basis, start, turned, held, partial, arrived, projected, kept, kept_pair, square, halves, crossed_two, core_parts, landed,
    load_sem, field_sem, cross_sem, pair_sem, trade_sem, core_sem, *sums
):
    place = Place(plane)
    gx, gy = place.gx, place.gy
    rows, cols, depth = field.shape
    place.greet()
    start[0] = start_one[...].T
    start[1] = start_two[...].T
    sums_one, sums_two = sums[: len(sums) // 2], sums[len(sums) // 2 :]
    sent = gram_one_sums(
        place, field, own, other, pair, pair_p, gram_pair, cross, crossed, load_sem, field_sem, cross_sem.at[0], sums_one[0]
    )
    sum_over_chips(place, *sums_one)
    unfold_sum(sums_one[3], terms)
    basis[...] = orthonormal(terms, start[0], held)
    pairs, trades, local = project(
        place, pair, basis, partial, arrived, projected, kept, pair_sem, trade_sem, cols, depth
    )
    own_one[...] = basis[:, pl.ds(pl.multiple_of(gx * rows, 128), rows)].T
    for copy in local:
        copy.wait()
    spread_kept(place, kept, kept_pair, gy, cols)
    for d in place.plane_order():
        for q in range(len(local)):
            trades[q, d].wait_recv()
        spread_kept(place, kept, kept_pair, place.plane_source(d), cols)
    sent.append(gram_two_sums(place, kept_pair, square, halves, crossed_two, cross_sem.at[1], sums_two[0]))
    sum_over_chips(place, *sums_two)
    unfold_sum(sums_two[3], terms)
    basis[...] = orthonormal(terms, start[1], held)
    whole_rows, part_ranks, part_depth = kept.shape
    splits = depth // part_depth
    each = core.shape[1]
    basis_high, basis_low = split(basis[...])
    both = jnp.concatenate([basis_high, basis_low], axis=0)
    order = place.plane_order()
    last = []
    for q in range(2):
        ranks = part_ranks // 2
        at = slice(q * ranks * part_depth, (q + 1) * ranks * part_depth)
        first = dot_nn(both, kept_pair[0:whole_rows, at])
        first = first[:RANK] + first[RANK:] + dot_nn(basis_high, kept_pair[whole_rows:, at])
        for r in range(ranks):
            core_parts[q * ranks + r] = first[:, r * part_depth : (r + 1) * part_depth]
        landing = landed.at[
            pl.ds(gy // splits * part_ranks + q * ranks, ranks),
            :,
            pl.ds(pl.multiple_of(gy % splits * part_depth, 128), part_depth),
        ]

        def piece(peer, q=q, ranks=ranks):
            return core_parts.at[q * ranks : (q + 1) * ranks, pl.ds(pl.multiple_of(peer * each, 8), each), :]

        for d in order:
            peer = place.plane_peer(d)
            last.append(remote(piece(peer), landing, core_sem.at[0, q, d], core_sem.at[1, q, d], {"gy": peer}))
        stays = pltpu.make_async_copy(piece(gy), landing, core_sem.at[0, q, 0])
        stays.start()
        local.append(stays)
    turned[...] = basis[...].T
    own_two[...] = turned[pl.ds(pl.multiple_of(gy * cols, 8), cols), :]
    for copy in sent + pairs + list(trades.values()):
        copy.wait_send()
    for copy in local[-2:]:
        copy.wait()
    for copy in last:
        copy.wait_recv()
    core[...] = landed[...]
    for copy in last:
        copy.wait_send()


def deliver(*refs):
    count = len(refs) // 2
    for k in range(count):
        refs[count + k][...] = refs[k][...]


def parts_of(cols):
    return [cols // 8, cols // 8, cols // 4, cols // 2]


def body(plane, field, start_one, start_two):
    rows, cols, depth = field.shape
    ny, nx, nz = plane
    planes = ny * nx
    splits = depth // 128
    part_ranks = RANK // 2 // (planes // splits)
    whole_rows = planes * cols
    half = whole_rows // 2
    parts = len(parts_of(cols))
    dma = pltpu.SemaphoreType.DMA
    vmem = pl.BlockSpec(memory_space=pltpu.VMEM)
    core_shape = (RANK // 2, RANK // planes, depth)
    size = max(2 * rows, whole_rows)
    outs = pl.pallas_call(
        functools.partial(kernel, plane),
        out_shape=(
            jax.ShapeDtypeStruct((rows, RANK), f32),
            jax.ShapeDtypeStruct((cols, RANK), f32),
            jax.ShapeDtypeStruct(core_shape, f32),
        ),
        in_specs=[pl.BlockSpec(memory_space=pl.ANY), vmem, vmem],
        out_specs=(vmem, vmem, vmem),
        scratch_shapes=[
            pltpu.VMEM((cols, rows, depth), f32),
            pltpu.VMEM((cols // 2, rows, depth), f32),
            pltpu.VMEM((2 * rows, cols * depth), bf16),
            pltpu.VMEM((2 * rows, cols // 2 * depth), bf16),
            pltpu.VMEM((2 * rows, rows), f32),
            pltpu.VMEM((rows, rows), f32),
            pltpu.VMEM((rows // 2, rows), f32),
            pltpu.VMEM((3, size, size), bf16),
            pltpu.VMEM((RANK, size), f32),
            pltpu.VMEM((2, RANK, size), f32),
            pltpu.VMEM((size, RANK), f32),
            pltpu.VMEM((RANK // 8, 9, 8, RANK), f32),
            pltpu.VMEM((cols, RANK, depth), f32),
            pltpu.VMEM((cols, RANK // 2, depth), f32),
            pltpu.VMEM((cols, RANK // 2, depth), f32),
            pltpu.VMEM((whole_rows, part_ranks, 128), f32),
            pltpu.VMEM((2 * whole_rows, part_ranks * 128), bf16),
            pltpu.VMEM((half, half), f32),
            pltpu.VMEM((2, half * 3 // 2, half), f32),
            pltpu.VMEM((half * 3 // 2, half), f32),
            pltpu.VMEM((part_ranks, RANK, 128), f32),
            pltpu.VMEM(core_shape, f32),
            dma((cols,)),
            dma((2, cols // 2)),
            dma((2, 2)),
            dma((2, parts)),
            dma((2, parts, planes)),
            dma((2, 2, planes)),
            *sum_scratch(plane, rows * 3 // 2, rows),
            *sum_scratch(plane, half * 3 // 2, half),
        ],
        compiler_params=pltpu.CompilerParams(collective_id=0, has_side_effects=True, vmem_limit_bytes=VMEM_LIMIT),
        name="hosvd",
    )(field, start_one, start_two)
    return pl.pallas_call(
        deliver,
        out_shape=tuple(jax.ShapeDtypeStruct(out.shape, f32) for out in outs),
        in_specs=[vmem] * len(outs),
        out_specs=(vmem,) * len(outs),
        name="deliver",
    )(*outs)


def solution(mesh):
    sizes = dict(mesh.shape)
    side = 4 if sizes["gy"] == 16 else 2
    plane = (sizes["gy"] // side, side, sizes["gz"])
    return jax.shard_map(
        functools.partial(body, plane),
        mesh=mesh,
        in_specs=(P("gx", "gy", "gz"), P(), P()),
        out_specs=(P("gx", None), P("gy", None), P("gx", "gy", "gz")),
        check_vma=False,
    )
```

```python
import functools

import jax
import jax.numpy as jnp
from jax import lax
from jax.experimental import pallas as pl
from jax.experimental.pallas import tpu as pltpu
from jax.sharding import PartitionSpec as P

RANK = 128
ITERS = 2
MESH = pl.DeviceIdType.MESH
f32 = jnp.float32
bf16 = jnp.bfloat16
highest = lax.Precision.HIGHEST
VMEM_LIMIT = 56 * 1024 * 1024


def split(value):
    high = value.astype(bf16)
    return high, (value - high.astype(f32)).astype(bf16)


def dot_nt(a, b, precision=None):
    return lax.dot_general(a, b, (((1,), (1,)), ((), ())), precision=precision, preferred_element_type=f32)


def dot_tn(a, b, precision=None):
    return lax.dot_general(a, b, (((0,), (0,)), ((), ())), precision=precision, preferred_element_type=f32)


def dot_nn(a, b, precision=None):
    return lax.dot_general(a, b, (((1,), (0,)), ((), ())), precision=precision, preferred_element_type=f32)


class Place:
    def __init__(self, plane):
        self.gx, self.gy, self.gz = (lax.axis_index(name) for name in ("gx", "gy", "gz"))
        self.partner = 1 - self.gx
        self.ny, self.nx, self.nz = plane
        self.np = self.ny * self.nx
        self.y, self.x = self.gy // self.nx, self.gy % self.nx

    def plane_peer(self, d):
        dy, dx = d // self.nx, d % self.nx
        return (self.y + dy) % self.ny * self.nx + (self.x + dx) % self.nx

    def plane_source(self, d):
        dy, dx = d // self.nx, d % self.nx
        return (self.y - dy) % self.ny * self.nx + (self.x - dx) % self.nx

    def plane_order(self):
        def hops(d):
            dy, dx = d // self.nx, d % self.nx
            return min(dy, self.ny - dy) + min(dx, self.nx - dx)

        return sorted(range(1, self.np), key=lambda d: (-hops(d), d))

    def z_peer(self, d):
        return (self.gz + d) % self.nz

    def others(self, kinds):
        found = []
        if "x" in kinds:
            found.append({"gx": self.partner})
        if "p" in kinds:
            found += [{"gy": self.plane_peer(d)} for d in range(1, self.np)]
        if "z" in kinds:
            found += [{"gz": self.z_peer(d)} for d in range(1, self.nz)]
        return found

    def greet(self):
        for peer in self.others("pzx"):
            pl.semaphore_signal(pltpu.get_barrier_semaphore(), inc=1, device_id=peer, device_id_type=MESH)

    def meet(self):
        pl.semaphore_wait(pltpu.get_barrier_semaphore(), len(self.others("pzx")))


def remote(src, dst, send_sem, recv_sem, device_id):
    copy = pltpu.make_async_remote_copy(
        src_ref=src, dst_ref=dst, send_sem=send_sem, recv_sem=recv_sem, device_id=device_id, device_id_type=MESH
    )
    copy.start()
    return copy


def sum_scratch(plane, rows, width):
    ny, nx, nz = plane
    planes = ny * nx
    chunk = rows // planes
    dma = pltpu.SemaphoreType.DMA
    return [
        pltpu.VMEM((rows, width), f32),
        pltpu.VMEM((planes, chunk, width), f32),
        pltpu.VMEM((nz, chunk, width), f32),
        pltpu.VMEM((2, rows, width), f32),
        dma((2, planes)),
        dma((2, nz)),
        dma((2, planes)),
        dma((2,)),
    ]


def sum_over_chips(place, total, parts, zparts, whole, rs_sem, z_sem, ag_sem, x_sem):
    chunk = total.shape[0] // place.np
    order = place.plane_order()
    sent = []
    for d in order:
        peer = place.plane_peer(d)
        piece = total.at[pl.ds(pl.multiple_of(peer * chunk, 8), chunk), :]
        sent.append(remote(piece, parts.at[d], rs_sem.at[0, d], rs_sem.at[1, d], {"gy": peer}))
    own = pl.ds(pl.multiple_of(place.gy * chunk, 8), chunk)
    value = total[own, :]
    for d, copy in list(zip(order, sent))[::-1]:
        copy.wait_recv()
        value = value + parts[d]
    zparts[place.gz] = value
    mine = zparts.at[place.gz]
    copies = [
        remote(mine, mine, z_sem.at[0, d], z_sem.at[1, d], {"gz": place.z_peer(d)})
        for d in sorted(range(1, place.nz), key=lambda d: -min(d, place.nz - d))
    ]
    for copy in copies:
        copy.wait_recv()
    value = zparts[0]
    for z in range(1, place.nz):
        value = value + zparts[z]
    whole[place.gx, own, :] = value
    sent += copies
    block = whole.at[place.gx, own, :]
    copies = [remote(block, block, ag_sem.at[0, d], ag_sem.at[1, d], {"gy": place.plane_peer(d)}) for d in order]
    for copy in copies:
        copy.wait_recv()
    mine = whole.at[place.gx]
    last = remote(mine, mine, x_sem.at[0], x_sem.at[1], {"gx": place.partner})
    for copy in sent + copies:
        copy.wait_send()
    last.wait()


PACKED = 5


def pack(packed, blocks, first=0):
    side = packed.shape[1]
    for k, block in enumerate(blocks, first):
        packed[k * side : (k + 1) * side, :] = block


def symmetric_blocks(plain, mixed):
    side = plain.shape[1] // 2
    one, two = slice(0, side), slice(side, 2 * side)
    return [plain[r, c] + mixed[r, c] + mixed[c, r].T for r, c in ((one, one), (one, two), (two, two))]


def unfold_sum(whole, terms):
    side = whole.shape[2]
    places = [[(0, 0), (0, 1), (1, 1), (0, 2), (0, 3)], [(2, 2), (2, 3), (3, 3), (1, 2), (1, 3)]]
    for half in range(2):
        for k, (i, j) in enumerate(places[half]):
            block = whole[half, k * side : (k + 1) * side, :]
            rows, cols = slice(i * side, (i + 1) * side), slice(j * side, (j + 1) * side)
            terms[0, rows, cols], terms[1, rows, cols], terms[2, rows, cols] = split3(block)
            if i != j:
                terms[0, cols, rows], terms[1, cols, rows], terms[2, cols, rows] = split3(block.T)


def eliminate(entry):
    n = len(entry)
    entry = [list(row) for row in entry]
    below = [[None] * n for _ in range(n)]
    pairs = []
    for k in range(0, n, 2):
        a, b, c = entry[k][k], entry[k + 1][k], entry[k + 1][k + 1]
        inverse = 1.0 / (a * c - b * b)
        pairs.append((a, b, c, inverse))
        factors = {}
        for i in range(k + 2, n):
            p, q = entry[i][k], entry[i][k + 1]
            factors[i] = (c * p - b * q) * inverse, (a * q - b * p) * inverse
        for i in range(k + 2, n):
            f, g = factors[i]
            for j in range(k + 2, i + 1):
                entry[i][j] = entry[i][j] - (f * entry[j][k] + g * entry[j][k + 1])
            for j in range(k):
                below[i][j] = below[i][j] - (f * below[k][j] + g * below[k + 1][j])
            below[i][k], below[i][k + 1] = -f, -g
    return below, pairs


def tree(terms):
    while len(terms) > 1:
        terms = [a + b for a, b in zip(terms[::2], terms[1::2])] + ([terms[-1]] if len(terms) % 2 else [])
    return terms[0]


def inverse_factor(crossed, held):
    n = crossed.shape[0]
    sub = lax.broadcasted_iota(jnp.int32, (8, n), 0)
    lane = lax.broadcasted_iota(jnp.int32, (8, n), 1)
    tiles = [crossed[8 * t : 8 * t + 8, :] for t in range(n // 8)]
    found = []

    def lanes_of(tile, k):
        return jnp.broadcast_to(tile[:, k : k + 1], (8, n))

    def row_of(t, which, k):
        return jnp.broadcast_to(held[t, which, k : k + 1, :], (8, n))

    for t in range(n // 8):
        first = 8 * t
        inside = (lane >= first) & (lane < first + 8)
        for k in range(8):
            held[t, k] = lanes_of(tiles[t], first + k)
        held[t, 8] = jnp.where(inside, jnp.where(lane == sub + first, 1.0, 0.0), tiles[t])
        below, pairs = eliminate([[row_of(t, j, i) for j in range(i + 1)] for i in range(8)])
        spread = [row_of(t, 8, k) for k in range(8)]
        rows = [
            tree([spread[i]] + [below[i][j] * spread[j] for j in range(i - i % 2)]) for i in range(8)
        ]
        value, scaled = None, []
        for m, (a, b, c, inverse) in enumerate(pairs):
            p, q = rows[2 * m], rows[2 * m + 1]
            scaled += [(c * p - b * q) * inverse, (a * q - b * p) * inverse]
            over = 1.0 / a
            first_row, second_row = p * lax.rsqrt(a), (q - (b * over) * p) * lax.rsqrt((a * c - b * b) * over)
            value = first_row if value is None else jnp.where(sub == 2 * m, first_row, value)
            value = jnp.where(sub == 2 * m + 1, second_row, value)
        found.append(jnp.where(lane < first + 8, value, 0.0))
        if t + 1 == n // 8:
            break
        solved = [
            tree([scaled[k]] + [below[i][k] * scaled[i] for i in range(k - k % 2 + 2, 8)]) for k in range(8)
        ]
        for u in range(t + 1, n // 8):
            terms = [lanes_of(tiles[u], first + k) * solved[k] for k in range(8)]
            tiles[u] = jnp.where(inside, 0.0, tiles[u]) - tree(terms)
    return jnp.concatenate(found, axis=0)


def split3(value):
    high = value.astype(bf16)
    rest = value - high.astype(f32)
    middle = rest.astype(bf16)
    return high, middle, (rest - middle.astype(f32)).astype(bf16)


def times(left, right):
    n = left.shape[0]
    high, middle, low = split3(left)
    one = dot_nn(jnp.concatenate([high, middle, low], axis=0), right[0])
    two = dot_nn(jnp.concatenate([high, middle], axis=0), right[1])
    three = dot_nn(high, right[2])
    return one[:n] + (one[n : 2 * n] + two[:n]) + (one[2 * n :] + two[n:] + three)


def square(rows):
    n = rows.shape[0]
    high, middle, low = split3(rows)
    one = dot_nt(jnp.concatenate([high, middle, low], axis=0), high)
    mid, last = one[n : 2 * n], one[2 * n :]
    return one[:n] + (mid + mid.T) + (last + last.T + dot_nt(middle, middle))


def orthonormal(terms, start, held):
    assert ITERS == 2
    product = times(start, terms)
    inverse = inverse_factor(square(product), held)
    second = times(product, terms)
    product = times(inverse, split3(second))
    return times(inverse_factor(square(product), held), split3(product))


def split_block(block, at, pair):
    rows = block.shape[0]
    pair[0:rows, at], pair[rows:, at] = split(block)


def gram_one_sums(place, field, own, other, pair, pair_p, gram, cross, crossed, load_sem, field_sem, cross_sem, total):
    rows, cols, depth = field.shape
    half = cols // 2
    gx, partner = place.gx, place.partner
    step = 8 * depth
    loads = []
    for j in range(cols):
        loads.append(pltpu.make_async_copy(field.at[:, j, :], own.at[j], load_sem.at[j]))
        loads[-1].start()
    gram[...] = jnp.zeros_like(gram)
    sends = []
    for c in range(cols // 8):
        for j in range(8 * c, 8 * c + 8):
            loads[j].wait()
            split_block(own[j], slice(j * depth, (j + 1) * depth), pair)
        at = slice(c * step, (c + 1) * step)
        gram[...] += dot_nt(pair[:, at], pair[0:rows, at])
        if c == 0:
            place.meet()
            for j in range(half):
                sends.append(
                    remote(
                        field.at[:, partner * half + j, :],
                        other.at[j],
                        field_sem.at[0, j],
                        field_sem.at[1, j],
                        {"gx": partner},
                    )
                )
    cross[...] = jnp.zeros_like(cross)
    for c in range(half // 8):
        for j in range(8 * c, 8 * c + 8):
            sends[j].wait_recv()
            split_block(other[j], slice(j * depth, (j + 1) * depth), pair_p)
        at = slice(c * step, (c + 1) * step)
        mine = pl.ds(pl.multiple_of(gx * half * depth + c * step, step), step)
        both = dot_nt(pair[:, mine], pair_p[0:rows, at])
        cross[...] += both[0:rows] + both[rows:] + dot_nt(pair[0:rows, mine], pair_p[rows:, at])
    value = cross[...]
    cross[...] = jnp.where(gx == 0, value, value.T)
    quarter = rows // 2
    copy = remote(
        cross.at[pl.ds(pl.multiple_of(partner * quarter, 8), quarter), :],
        crossed,
        cross_sem.at[0],
        cross_sem.at[1],
        {"gx": partner},
    )
    pack(total, symmetric_blocks(gram.at[0:rows, :], gram.at[rows:, :]))
    copy.wait_recv()
    strip = cross[pl.ds(pl.multiple_of(gx * quarter, 8), quarter), :] + crossed[...]
    pack(total, [strip[:, 0:quarter], strip[:, quarter:]], 3)
    return sends + [copy]


def project(place, pair, basis, partial, arrived, projected, kept, pair_sem, trade_sem, cols, depth):
    gx, gy, partner = place.gx, place.gy, place.partner
    rows = pair.shape[0] // 2
    ranks = RANK // 2
    sizes = parts_of(cols)
    spans = [slice(sum(sizes[:q]), sum(sizes[: q + 1])) for q in range(len(sizes))]
    _, part_ranks, part_depth = kept.shape
    splits = depth // part_depth
    basis_high, basis_low = split(basis[:, pl.ds(pl.multiple_of(gx * rows, 128), rows)])
    both = jnp.concatenate([basis_high, basis_low], axis=0)
    here = pl.ds(pl.multiple_of(gx * ranks, 8), ranks)
    there = pl.ds(pl.multiple_of(partner * ranks, 8), ranks)

    def piece(q, peer):
        return projected.at[
            spans[q],
            pl.ds(pl.multiple_of(peer // splits * part_ranks, 8), part_ranks),
            pl.ds(pl.multiple_of(peer % splits * part_depth, 128), part_depth),
        ]

    def landing(q):
        return kept.at[pl.ds(gy * cols + spans[q].start, sizes[q]), :, :]

    def partials(q):
        for j in range(spans[q].start, spans[q].stop):
            at = slice(j * depth, (j + 1) * depth)
            first = dot_nn(both, pair[0:rows, at])
            partial[j] = first[:RANK] + first[RANK:] + dot_nn(basis_high, pair[rows:, at])
        at = spans[q]
        return remote(partial.at[at, there, :], arrived.at[at], pair_sem.at[0, q], pair_sem.at[1, q], {"gx": partner})

    order = place.plane_order()
    pairs, trades = [partials(0)], {}
    for q in range(len(sizes)):
        if q + 1 < len(sizes):
            pairs.append(partials(q + 1))
        pairs[q].wait_recv()
        for j in range(spans[q].start, spans[q].stop):
            projected[j] = partial[j, here, :] + arrived[j]
        for d in order:
            peer = place.plane_peer(d)
            trades[q, d] = remote(
                piece(q, peer), landing(q), trade_sem.at[0, q, d], trade_sem.at[1, q, d], {"gy": peer}
            )
    local = []
    for q in range(len(sizes)):
        local.append(pltpu.make_async_copy(piece(q, gy), landing(q), trade_sem.at[0, q, 0]))
        local[-1].start()
    return pairs, trades, local


def spread_kept(place, kept, kept_pair, peer, cols):
    whole_rows, part_ranks, lanes = kept.shape
    flat = kept.reshape(whole_rows * part_ranks, lanes)
    for r in range(part_ranks):
        value = flat[pl.ds(peer * cols * part_ranks + r, cols, stride=part_ranks), :]
        at = slice(r * lanes, (r + 1) * lanes)
        first = pl.ds(pl.multiple_of(peer * cols, 16), cols)
        second = pl.ds(pl.multiple_of(whole_rows + peer * cols, 16), cols)
        kept_pair[first, at], kept_pair[second, at] = split(value)


def gram_two_sums(place, kept_pair, plain, mixed, halves, crossed, cross_sem, total):
    whole_rows = kept_pair.shape[0] // 2
    half = whole_rows // 2
    side = half // 2
    partner = {"gx": place.partner}
    for k in range(2):
        high = kept_pair[half * k : half * (k + 1), :]
        mixed[...] = dot_nt(kept_pair[whole_rows + half * k : whole_rows + half * (k + 1), :], high)
        plain[...] = dot_nt(high, high)
        pack(halves.at[k], symmetric_blocks(plain, mixed))
    head, tail = slice(0, 3 * side), slice(3 * side, 5 * side)
    copies = [remote(halves.at[place.partner, head, :], crossed.at[head, :], cross_sem.at[0, 0], cross_sem.at[1, 0], partner)]
    high, low = kept_pair[0:half, :], kept_pair[whole_rows : whole_rows + half, :]
    plain[...] = dot_nt(high, kept_pair[half:whole_rows, :])
    plain[...] += dot_nt(low, kept_pair[half:whole_rows, :])
    plain[...] += dot_nt(high, kept_pair[whole_rows + half :, :])
    for k in range(2):
        rows = slice(k * side, (k + 1) * side)
        pack(halves.at[k], [plain[rows, 0:side], plain[rows, side:]], 3)
    copies.append(remote(halves.at[place.partner, tail, :], crossed.at[tail, :], cross_sem.at[0, 1], cross_sem.at[1, 1], partner))
    for copy, at in zip(copies, (head, tail)):
        copy.wait_recv()
        total[at, :] = halves[place.gx, at, :] + crossed[at, :]
    return copies


def kernel(
    plane, field, start_one, start_two, own_one, own_two, core, own, other, pair, pair_p, gram_pair, cross, crossed,
    terms, basis, start, turned, held, partial, arrived, projected, kept, kept_pair, plain, mixed, halves, crossed_two, core_parts, landed,
    load_sem, field_sem, cross_sem, cross_two_sem, pair_sem, trade_sem, core_sem, *sums
):
    place = Place(plane)
    gx, gy = place.gx, place.gy
    rows, cols, depth = field.shape
    place.greet()
    start[0] = start_one[...].T
    start[1] = start_two[...].T
    sums_one, sums_two = sums[: len(sums) // 2], sums[len(sums) // 2 :]
    sent = gram_one_sums(
        place, field, own, other, pair, pair_p, gram_pair, cross, crossed, load_sem, field_sem, cross_sem, sums_one[0]
    )
    sum_over_chips(place, *sums_one)
    unfold_sum(sums_one[3], terms)
    basis[...] = orthonormal(terms, start[0], held)
    pairs, trades, local = project(
        place, pair, basis, partial, arrived, projected, kept, pair_sem, trade_sem, cols, depth
    )
    own_one[...] = basis[:, pl.ds(pl.multiple_of(gx * rows, 128), rows)].T
    for copy in local:
        copy.wait()
    spread_kept(place, kept, kept_pair, gy, cols)
    for d in place.plane_order():
        for q in range(len(local)):
            trades[q, d].wait_recv()
        spread_kept(place, kept, kept_pair, place.plane_source(d), cols)
    sent += gram_two_sums(place, kept_pair, plain, mixed, halves, crossed_two, cross_two_sem, sums_two[0])
    sum_over_chips(place, *sums_two)
    unfold_sum(sums_two[3], terms)
    basis[...] = orthonormal(terms, start[1], held)
    whole_rows, part_ranks, part_depth = kept.shape
    splits = depth // part_depth
    each = core.shape[1]
    basis_high, basis_low = split(basis[...])
    both = jnp.concatenate([basis_high, basis_low], axis=0)
    order = place.plane_order()
    last = []
    for q in range(CORE_PARTS):
        ranks = part_ranks // CORE_PARTS
        at = slice(q * ranks * part_depth, (q + 1) * ranks * part_depth)
        first = dot_nn(both, kept_pair[0:whole_rows, at])
        first = first[:RANK] + first[RANK:] + dot_nn(basis_high, kept_pair[whole_rows:, at])
        for r in range(ranks):
            core_parts[q * ranks + r] = first[:, r * part_depth : (r + 1) * part_depth]
        landing = landed.at[
            pl.ds(gy // splits * part_ranks + q * ranks, ranks),
            :,
            pl.ds(pl.multiple_of(gy % splits * part_depth, 128), part_depth),
        ]

        def piece(peer, q=q, ranks=ranks):
            return core_parts.at[q * ranks : (q + 1) * ranks, pl.ds(pl.multiple_of(peer * each, 8), each), :]

        for d in order:
            peer = place.plane_peer(d)
            last.append(remote(piece(peer), landing, core_sem.at[0, q, d], core_sem.at[1, q, d], {"gy": peer}))
        stays = pltpu.make_async_copy(piece(gy), landing, core_sem.at[0, q, 0])
        stays.start()
        local.append(stays)
    turned[...] = basis[...].T
    own_two[...] = turned[pl.ds(pl.multiple_of(gy * cols, 8), cols), :]
    for copy in sent + pairs + list(trades.values()):
        copy.wait_send()
    for copy in local[-CORE_PARTS:]:
        copy.wait()
    for copy in last:
        copy.wait_recv()
    core[...] = landed[...]
    for copy in last:
        copy.wait_send()


def deliver(*refs):
    count = len(refs) // 2
    for k in range(count):
        refs[count + k][...] = refs[k][...]


CORE_PARTS = 1


def parts_of(cols):
    return [cols // 4, cols * 3 // 4]


def body(plane, field, start_one, start_two):
    rows, cols, depth = field.shape
    ny, nx, nz = plane
    planes = ny * nx
    splits = depth // 128
    part_ranks = RANK // 2 // (planes // splits)
    whole_rows = planes * cols
    half = whole_rows // 2
    parts = len(parts_of(cols))
    dma = pltpu.SemaphoreType.DMA
    vmem = pl.BlockSpec(memory_space=pltpu.VMEM)
    core_shape = (RANK // 2, RANK // planes, depth)
    size = max(2 * rows, whole_rows)
    outs = pl.pallas_call(
        functools.partial(kernel, plane),
        out_shape=(
            jax.ShapeDtypeStruct((rows, RANK), f32),
            jax.ShapeDtypeStruct((cols, RANK), f32),
            jax.ShapeDtypeStruct(core_shape, f32),
        ),
        in_specs=[pl.BlockSpec(memory_space=pl.ANY), vmem, vmem],
        out_specs=(vmem, vmem, vmem),
        scratch_shapes=[
            pltpu.VMEM((cols, rows, depth), f32),
            pltpu.VMEM((cols // 2, rows, depth), f32),
            pltpu.VMEM((2 * rows, cols * depth), bf16),
            pltpu.VMEM((2 * rows, cols // 2 * depth), bf16),
            pltpu.VMEM((2 * rows, rows), f32),
            pltpu.VMEM((rows, rows), f32),
            pltpu.VMEM((rows // 2, rows), f32),
            pltpu.VMEM((3, size, size), bf16),
            pltpu.VMEM((RANK, size), f32),
            pltpu.VMEM((2, RANK, size), f32),
            pltpu.VMEM((size, RANK), f32),
            pltpu.VMEM((RANK // 8, 9, 8, RANK), f32),
            pltpu.VMEM((cols, RANK, depth), f32),
            pltpu.VMEM((cols, RANK // 2, depth), f32),
            pltpu.VMEM((cols, RANK // 2, depth), f32),
            pltpu.VMEM((whole_rows, part_ranks, 128), f32),
            pltpu.VMEM((2 * whole_rows, part_ranks * 128), bf16),
            pltpu.VMEM((half, half), f32),
            pltpu.VMEM((half, half), f32),
            pltpu.VMEM((2, PACKED * half // 2, half // 2), f32),
            pltpu.VMEM((PACKED * half // 2, half // 2), f32),
            pltpu.VMEM((part_ranks, RANK, 128), f32),
            pltpu.VMEM(core_shape, f32),
            dma((cols,)),
            dma((2, cols // 2)),
            dma((2,)),
            dma((2, 2)),
            dma((2, parts)),
            dma((2, parts, planes)),
            dma((2, CORE_PARTS, planes)),
            *sum_scratch(plane, PACKED * rows // 2, rows // 2),
            *sum_scratch(plane, PACKED * half // 2, half // 2),
        ],
        compiler_params=pltpu.CompilerParams(collective_id=0, has_side_effects=True, vmem_limit_bytes=VMEM_LIMIT),
        name="hosvd",
    )(field, start_one, start_two)
    return pl.pallas_call(
        deliver,
        out_shape=tuple(jax.ShapeDtypeStruct(out.shape, f32) for out in outs),
        in_specs=[vmem] * len(outs),
        out_specs=(vmem,) * len(outs),
        name="deliver",
    )(*outs)


def solution(mesh):
    sizes = dict(mesh.shape)
    side = 4 if sizes["gy"] == 16 else 2
    plane = (sizes["gy"] // side, side, sizes["gz"])
    return jax.shard_map(
        functools.partial(body, plane),
        mesh=mesh,
        in_specs=(P("gx", "gy", "gz"), P(), P()),
        out_specs=(P("gx", None), P("gy", None), P("gx", "gy", "gz")),
        check_vma=False,
    )
```

```python
import functools

import jax
import jax.numpy as jnp
from jax import lax
from jax.experimental import pallas as pl
from jax.experimental.pallas import tpu as pltpu
from jax.sharding import PartitionSpec as P

RANK = 128
ITERS = 2
MESH = pl.DeviceIdType.MESH
f32 = jnp.float32
bf16 = jnp.bfloat16
highest = lax.Precision.HIGHEST
VMEM_LIMIT = 56 * 1024 * 1024


def split(value):
    high = value.astype(bf16)
    return high, (value - high.astype(f32)).astype(bf16)


def dot_nt(a, b, precision=None):
    return lax.dot_general(a, b, (((1,), (1,)), ((), ())), precision=precision, preferred_element_type=f32)


def dot_tn(a, b, precision=None):
    return lax.dot_general(a, b, (((0,), (0,)), ((), ())), precision=precision, preferred_element_type=f32)


def dot_nn(a, b, precision=None):
    return lax.dot_general(a, b, (((1,), (0,)), ((), ())), precision=precision, preferred_element_type=f32)


class Place:
    def __init__(self, plane):
        self.gx, self.gy, self.gz = (lax.axis_index(name) for name in ("gx", "gy", "gz"))
        self.partner = 1 - self.gx
        self.ny, self.nx, self.nz = plane
        self.np = self.ny * self.nx
        self.y, self.x = self.gy // self.nx, self.gy % self.nx

    def plane_peer(self, d):
        dy, dx = d // self.nx, d % self.nx
        return (self.y + dy) % self.ny * self.nx + (self.x + dx) % self.nx

    def plane_source(self, d):
        dy, dx = d // self.nx, d % self.nx
        return (self.y - dy) % self.ny * self.nx + (self.x - dx) % self.nx

    def plane_order(self):
        def hops(d):
            dy, dx = d // self.nx, d % self.nx
            return min(dy, self.ny - dy) + min(dx, self.nx - dx)

        return sorted(range(1, self.np), key=lambda d: (-hops(d), d))

    def z_peer(self, d):
        return (self.gz + d) % self.nz

    def others(self, kinds):
        found = []
        if "x" in kinds:
            found.append({"gx": self.partner})
        if "p" in kinds:
            found += [{"gy": self.plane_peer(d)} for d in range(1, self.np)]
        if "z" in kinds:
            found += [{"gz": self.z_peer(d)} for d in range(1, self.nz)]
        return found

    def greet(self):
        for peer in self.others("pzx"):
            pl.semaphore_signal(pltpu.get_barrier_semaphore(), inc=1, device_id=peer, device_id_type=MESH)

    def meet(self):
        pl.semaphore_wait(pltpu.get_barrier_semaphore(), len(self.others("pzx")))


def remote(src, dst, send_sem, recv_sem, device_id):
    copy = pltpu.make_async_remote_copy(
        src_ref=src, dst_ref=dst, send_sem=send_sem, recv_sem=recv_sem, device_id=device_id, device_id_type=MESH
    )
    copy.start()
    return copy


def sum_scratch(plane, rows, width):
    ny, nx, nz = plane
    planes = ny * nx
    chunk = rows // planes
    dma = pltpu.SemaphoreType.DMA
    return [
        pltpu.VMEM((rows, width), f32),
        pltpu.VMEM((planes, chunk, width), f32),
        pltpu.VMEM((nz, chunk, width), f32),
        pltpu.VMEM((2, rows, width), f32),
        dma((2, planes)),
        dma((2, nz)),
        dma((2, planes)),
        dma((2,)),
    ]


def sum_over_chips(place, total, parts, zparts, whole, rs_sem, z_sem, ag_sem, x_sem, meanwhile=None):
    chunk = total.shape[0] // place.np
    order = place.plane_order()
    sent = []
    for d in order:
        peer = place.plane_peer(d)
        piece = total.at[pl.ds(pl.multiple_of(peer * chunk, 8), chunk), :]
        sent.append(remote(piece, parts.at[d], rs_sem.at[0, d], rs_sem.at[1, d], {"gy": peer}))
    if meanwhile:
        meanwhile()
    own = pl.ds(pl.multiple_of(place.gy * chunk, 8), chunk)
    value = total[own, :]
    for d, copy in list(zip(order, sent))[::-1]:
        copy.wait_recv()
        value = value + parts[d]
    zparts[place.gz] = value
    mine = zparts.at[place.gz]
    copies = [
        remote(mine, mine, z_sem.at[0, d], z_sem.at[1, d], {"gz": place.z_peer(d)})
        for d in sorted(range(1, place.nz), key=lambda d: -min(d, place.nz - d))
    ]
    for copy in copies:
        copy.wait_recv()
    value = zparts[0]
    for z in range(1, place.nz):
        value = value + zparts[z]
    whole[place.gx, own, :] = value
    sent += copies
    block = whole.at[place.gx, own, :]
    copies = [remote(block, block, ag_sem.at[0, d], ag_sem.at[1, d], {"gy": place.plane_peer(d)}) for d in order]
    for copy in copies:
        copy.wait_recv()
    mine = whole.at[place.gx]
    last = remote(mine, mine, x_sem.at[0], x_sem.at[1], {"gx": place.partner})
    for copy in sent + copies:
        copy.wait_send()
    last.wait()


PACKED = 5


def pack(packed, blocks, first=0):
    side = packed.shape[1]
    for k, block in enumerate(blocks, first):
        packed[k * side : (k + 1) * side, :] = block


def symmetric_blocks(plain, mixed):
    side = plain.shape[1] // 2
    one, two = slice(0, side), slice(side, 2 * side)
    return [plain[r, c] + mixed[r, c] + mixed[c, r].T for r, c in ((one, one), (one, two), (two, two))]


def unfold_sum(whole, terms):
    side = whole.shape[2]
    places = [[(0, 0), (0, 1), (1, 1), (0, 2), (0, 3)], [(2, 2), (2, 3), (3, 3), (1, 2), (1, 3)]]
    for half in range(2):
        for k, (i, j) in enumerate(places[half]):
            block = whole[half, k * side : (k + 1) * side, :]
            rows, cols = slice(i * side, (i + 1) * side), slice(j * side, (j + 1) * side)
            terms[0, rows, cols], terms[1, rows, cols], terms[2, rows, cols] = split3(block)
            if i != j:
                terms[0, cols, rows], terms[1, cols, rows], terms[2, cols, rows] = split3(block.T)


def eliminate(entry):
    n = len(entry)
    entry = [list(row) for row in entry]
    below = [[None] * n for _ in range(n)]
    pairs = []
    for k in range(0, n, 2):
        a, b, c = entry[k][k], entry[k + 1][k], entry[k + 1][k + 1]
        inverse = 1.0 / (a * c - b * b)
        pairs.append((a, b, c, inverse))
        factors = {}
        for i in range(k + 2, n):
            p, q = entry[i][k], entry[i][k + 1]
            factors[i] = (c * p - b * q) * inverse, (a * q - b * p) * inverse
        for i in range(k + 2, n):
            f, g = factors[i]
            for j in range(k + 2, i + 1):
                entry[i][j] = entry[i][j] - (f * entry[j][k] + g * entry[j][k + 1])
            for j in range(k):
                below[i][j] = below[i][j] - (f * below[k][j] + g * below[k + 1][j])
            below[i][k], below[i][k + 1] = -f, -g
    return below, pairs


def tree(terms):
    while len(terms) > 1:
        terms = [a + b for a, b in zip(terms[::2], terms[1::2])] + ([terms[-1]] if len(terms) % 2 else [])
    return terms[0]


def inverse_factor(crossed, held):
    n = crossed.shape[0]
    sub = lax.broadcasted_iota(jnp.int32, (8, n), 0)
    lane = lax.broadcasted_iota(jnp.int32, (8, n), 1)
    tiles = [crossed[8 * t : 8 * t + 8, :] for t in range(n // 8)]
    found = []

    def lanes_of(tile, k):
        return jnp.broadcast_to(tile[:, k : k + 1], (8, n))

    def row_of(t, which, k):
        return jnp.broadcast_to(held[t, which, k : k + 1, :], (8, n))

    for t in range(n // 8):
        first = 8 * t
        inside = (lane >= first) & (lane < first + 8)
        for k in range(8):
            held[t, k] = lanes_of(tiles[t], first + k)
        held[t, 8] = jnp.where(inside, jnp.where(lane == sub + first, 1.0, 0.0), tiles[t])
        below, pairs = eliminate([[row_of(t, j, i) for j in range(i + 1)] for i in range(8)])
        spread = [row_of(t, 8, k) for k in range(8)]
        rows = [
            tree([spread[i]] + [below[i][j] * spread[j] for j in range(i - i % 2)]) for i in range(8)
        ]
        value, scaled = None, []
        for m, (a, b, c, inverse) in enumerate(pairs):
            p, q = rows[2 * m], rows[2 * m + 1]
            scaled += [(c * p - b * q) * inverse, (a * q - b * p) * inverse]
            over = 1.0 / a
            first_row, second_row = p * lax.rsqrt(a), (q - (b * over) * p) * lax.rsqrt((a * c - b * b) * over)
            value = first_row if value is None else jnp.where(sub == 2 * m, first_row, value)
            value = jnp.where(sub == 2 * m + 1, second_row, value)
        found.append(jnp.where(lane < first + 8, value, 0.0))
        if t + 1 == n // 8:
            break
        solved = [
            tree([scaled[k]] + [below[i][k] * scaled[i] for i in range(k - k % 2 + 2, 8)]) for k in range(8)
        ]
        for u in range(t + 1, n // 8):
            terms = [lanes_of(tiles[u], first + k) * solved[k] for k in range(8)]
            tiles[u] = jnp.where(inside, 0.0, tiles[u]) - tree(terms)
    return jnp.concatenate(found, axis=0)


def split3(value):
    high = value.astype(bf16)
    rest = value - high.astype(f32)
    middle = rest.astype(bf16)
    return high, middle, (rest - middle.astype(f32)).astype(bf16)


def times(left, right):
    n = left.shape[0]
    high, middle, low = split3(left)
    one = dot_nn(jnp.concatenate([high, middle, low], axis=0), right[0])
    two = dot_nn(jnp.concatenate([high, middle], axis=0), right[1])
    three = dot_nn(high, right[2])
    return one[:n] + (one[n : 2 * n] + two[:n]) + (one[2 * n :] + two[n:] + three)


def square(rows):
    n = rows.shape[0]
    high, middle, low = split3(rows)
    one = dot_nt(jnp.concatenate([high, middle, low], axis=0), high)
    mid, last = one[n : 2 * n], one[2 * n :]
    return one[:n] + (mid + mid.T) + (last + last.T + dot_nt(middle, middle))


def orthonormal(terms, start, held):
    assert ITERS == 2
    product = times(start, terms)
    inverse = inverse_factor(square(product), held)
    second = times(product, terms)
    product = times(inverse, split3(second))
    return times(inverse_factor(square(product), held), split3(product))


def split_block(block, at, pair):
    rows = block.shape[0]
    pair[0:rows, at], pair[rows:, at] = split(block)


def gram_one_sums(place, field, own, other, pair, pair_p, gram, cross, crossed, load_sem, field_sem, cross_sem, total):
    rows, cols, depth = field.shape
    half = cols // 2
    gx, partner = place.gx, place.partner
    step = 8 * depth
    loads = []
    for j in range(cols):
        loads.append(pltpu.make_async_copy(field.at[:, j, :], own.at[j], load_sem.at[j]))
        loads[-1].start()
    gram[...] = jnp.zeros_like(gram)
    sends = []
    for c in range(cols // 8):
        for j in range(8 * c, 8 * c + 8):
            loads[j].wait()
            split_block(own[j], slice(j * depth, (j + 1) * depth), pair)
        at = slice(c * step, (c + 1) * step)
        gram[...] += dot_nt(pair[:, at], pair[0:rows, at])
        if c == 0:
            place.meet()
            for j in range(half):
                sends.append(
                    remote(
                        field.at[:, partner * half + j, :],
                        other.at[j],
                        field_sem.at[0, j],
                        field_sem.at[1, j],
                        {"gx": partner},
                    )
                )
    cross[...] = jnp.zeros_like(cross)
    step = 4 * depth
    for c in range(half // 4):
        for j in range(4 * c, 4 * c + 4):
            sends[j].wait_recv()
            split_block(other[j], slice(j * depth, (j + 1) * depth), pair_p)
        at = slice(c * step, (c + 1) * step)
        mine = pl.ds(pl.multiple_of(gx * half * depth + c * step, step), step)
        both = dot_nt(pair[:, mine], pair_p[0:rows, at])
        cross[...] += both[0:rows] + both[rows:] + dot_nt(pair[0:rows, mine], pair_p[rows:, at])
    value = cross[...]
    cross[...] = jnp.where(gx == 0, value, value.T)
    quarter = rows // 2
    copy = remote(
        cross.at[pl.ds(pl.multiple_of(partner * quarter, 8), quarter), :],
        crossed,
        cross_sem.at[0],
        cross_sem.at[1],
        {"gx": partner},
    )
    pack(total, symmetric_blocks(gram.at[0:rows, :], gram.at[rows:, :]))
    copy.wait_recv()
    strip = cross[pl.ds(pl.multiple_of(gx * quarter, 8), quarter), :] + crossed[...]
    pack(total, [strip[:, 0:quarter], strip[:, quarter:]], 3)
    return sends + [copy]


def project(place, pair, basis, partial, arrived, projected, kept, pair_sem, trade_sem, cols, depth):
    gx, gy, partner = place.gx, place.gy, place.partner
    rows = pair.shape[0] // 2
    ranks = RANK // 2
    sizes = parts_of(cols)
    spans = [slice(sum(sizes[:q]), sum(sizes[: q + 1])) for q in range(len(sizes))]
    _, part_ranks, part_depth = kept.shape
    splits = depth // part_depth
    basis_high, basis_low = split(basis[:, pl.ds(pl.multiple_of(gx * rows, 128), rows)])
    both = jnp.concatenate([basis_high, basis_low], axis=0)
    here = pl.ds(pl.multiple_of(gx * ranks, 8), ranks)
    there = pl.ds(pl.multiple_of(partner * ranks, 8), ranks)

    def piece(q, peer):
        return projected.at[
            spans[q],
            pl.ds(pl.multiple_of(peer // splits * part_ranks, 8), part_ranks),
            pl.ds(pl.multiple_of(peer % splits * part_depth, 128), part_depth),
        ]

    def landing(q):
        return kept.at[pl.ds(gy * cols + spans[q].start, sizes[q]), :, :]

    def partials(q):
        for j in range(spans[q].start, spans[q].stop):
            at = slice(j * depth, (j + 1) * depth)
            first = dot_nn(both, pair[0:rows, at])
            partial[j] = first[:RANK] + first[RANK:] + dot_nn(basis_high, pair[rows:, at])
        at = spans[q]
        return remote(partial.at[at, there, :], arrived.at[at], pair_sem.at[0, q], pair_sem.at[1, q], {"gx": partner})

    order = place.plane_order()
    pairs, trades = [partials(0)], {}
    for q in range(len(sizes)):
        if q + 1 < len(sizes):
            pairs.append(partials(q + 1))
        pairs[q].wait_recv()
        for j in range(spans[q].start, spans[q].stop):
            projected[j] = partial[j, here, :] + arrived[j]
        for d in order:
            peer = place.plane_peer(d)
            trades[q, d] = remote(
                piece(q, peer), landing(q), trade_sem.at[0, q, d], trade_sem.at[1, q, d], {"gy": peer}
            )
    local = []
    for q in range(len(sizes)):
        local.append(pltpu.make_async_copy(piece(q, gy), landing(q), trade_sem.at[0, q, 0]))
        local[-1].start()
    return pairs, trades, local


def spread_kept(kept, kept_pair, start, count):
    whole_rows, part_ranks, lanes = kept.shape
    flat = kept.reshape(whole_rows * part_ranks, lanes)
    for r in range(part_ranks):
        value = flat[pl.ds(start * part_ranks + r, count, stride=part_ranks), :]
        at = slice(r * lanes, (r + 1) * lanes)
        first = pl.ds(pl.multiple_of(start, 16), count)
        second = pl.ds(pl.multiple_of(whole_rows + start, 16), count)
        kept_pair[first, at], kept_pair[second, at] = split(value)


def gram_two_sums(place, kept_pair, plain, mixed, halves, crossed, cross_sem, total):
    whole_rows = kept_pair.shape[0] // 2
    half = whole_rows // 2
    side = half // 2
    partner = {"gx": place.partner}
    for k in range(2):
        high = kept_pair[half * k : half * (k + 1), :]
        mixed[...] = dot_nt(kept_pair[whole_rows + half * k : whole_rows + half * (k + 1), :], high)
        plain[...] = dot_nt(high, high)
        pack(halves.at[k], symmetric_blocks(plain, mixed))
    head, tail = slice(0, 3 * side), slice(3 * side, 5 * side)
    copies = [remote(halves.at[place.partner, head, :], crossed.at[head, :], cross_sem.at[0, 0], cross_sem.at[1, 0], partner)]
    high, low = kept_pair[0:half, :], kept_pair[whole_rows : whole_rows + half, :]
    plain[...] = dot_nt(high, kept_pair[half:whole_rows, :])
    plain[...] += dot_nt(low, kept_pair[half:whole_rows, :])
    plain[...] += dot_nt(high, kept_pair[whole_rows + half :, :])
    for k in range(2):
        rows = slice(k * side, (k + 1) * side)
        pack(halves.at[k], [plain[rows, 0:side], plain[rows, side:]], 3)
    copies.append(remote(halves.at[place.partner, tail, :], crossed.at[tail, :], cross_sem.at[0, 1], cross_sem.at[1, 1], partner))
    for copy, at in zip(copies, (head, tail)):
        copy.wait_recv()
        total[at, :] = halves[place.gx, at, :] + crossed[at, :]
    return copies


def kernel(
    plane, field, start_one, start_two, own_one, own_two, core, own, other, pair, pair_p, gram_pair, cross, crossed,
    terms, basis, raw, start, rows_one, turned, held, partial, arrived, projected, kept, kept_pair, plain, mixed, halves, crossed_two, core_parts, landed,
    load_sem, start_sem, field_sem, cross_sem, cross_two_sem, pair_sem, trade_sem, core_sem, out_sem, *sums
):
    place = Place(plane)
    gx, gy = place.gx, place.gy
    rows, cols, depth = field.shape
    place.greet()
    start_loads = [
        pltpu.make_async_copy(given, raw.at[k], start_sem.at[k]) for k, given in enumerate((start_one, start_two))
    ]
    for copy in start_loads:
        copy.start()

    def turn_starts():
        for k, copy in enumerate(start_loads):
            copy.wait()
            start[k] = raw[k].T

    sums_one, sums_two = sums[: len(sums) // 2], sums[len(sums) // 2 :]
    sent = gram_one_sums(
        place, field, own, other, pair, pair_p, gram_pair, cross, crossed, load_sem, field_sem, cross_sem, sums_one[0]
    )
    sum_over_chips(place, *sums_one, meanwhile=turn_starts)
    unfold_sum(sums_one[3], terms)
    basis[...] = orthonormal(terms, start[0], held)
    pairs, trades, local = project(
        place, pair, basis, partial, arrived, projected, kept, pair_sem, trade_sem, cols, depth
    )
    rows_one[...] = basis[:, pl.ds(pl.multiple_of(gx * rows, 128), rows)].T
    outs = [pltpu.make_async_copy(rows_one, own_one, out_sem.at[0])]
    outs[0].start()
    for copy in local:
        copy.wait()
    spread_kept(kept, kept_pair, gy * cols, cols)
    for k, some in enumerate(((0, 1), (2,))):
        for d in place.plane_order():
            for q in some:
                trades[q, d].wait_recv()
            spread_kept(kept, kept_pair, place.plane_source(d) * cols + k * (cols // 2), cols // 2)
    sent += gram_two_sums(place, kept_pair, plain, mixed, halves, crossed_two, cross_two_sem, sums_two[0])
    sum_over_chips(place, *sums_two)
    unfold_sum(sums_two[3], terms)
    basis[...] = orthonormal(terms, start[1], held)
    whole_rows, part_ranks, part_depth = kept.shape
    splits = depth // part_depth
    each = landed.shape[1]
    basis_high, basis_low = split(basis[...])
    both = jnp.concatenate([basis_high, basis_low], axis=0)
    order = place.plane_order()
    last = []
    for q in range(CORE_PARTS):
        ranks = part_ranks // CORE_PARTS
        at = slice(q * ranks * part_depth, (q + 1) * ranks * part_depth)
        first = dot_nn(both, kept_pair[0:whole_rows, at])
        first = first[:RANK] + first[RANK:] + dot_nn(basis_high, kept_pair[whole_rows:, at])
        for r in range(ranks):
            core_parts[q * ranks + r] = first[:, r * part_depth : (r + 1) * part_depth]
        landing = landed.at[
            pl.ds(gy // splits * part_ranks + q * ranks, ranks),
            :,
            pl.ds(pl.multiple_of(gy % splits * part_depth, 128), part_depth),
        ]

        def piece(peer, q=q, ranks=ranks):
            return core_parts.at[q * ranks : (q + 1) * ranks, pl.ds(pl.multiple_of(peer * each, 8), each), :]

        for d in order:
            peer = place.plane_peer(d)
            last.append(remote(piece(peer), landing, core_sem.at[0, q, d], core_sem.at[1, q, d], {"gy": peer}))
        stays = pltpu.make_async_copy(piece(gy), landing, core_sem.at[0, q, 0])
        stays.start()
        local.append(stays)
    turned[...] = basis[...].T
    outs.append(pltpu.make_async_copy(turned.at[pl.ds(pl.multiple_of(gy * cols, 8), cols), :], own_two, out_sem.at[1]))
    outs[1].start()
    for copy in sent + pairs + list(trades.values()):
        copy.wait_send()
    for copy in local[-CORE_PARTS:]:
        copy.wait()
    for copy in last:
        copy.wait_recv()
    outs.append(pltpu.make_async_copy(landed, core, out_sem.at[2]))
    outs[2].start()
    for copy in last:
        copy.wait_send()
    for copy in outs:
        copy.wait()


def deliver(*refs):
    count = len(refs) // 2
    for k in range(count):
        refs[count + k][...] = refs[k][...]


CORE_PARTS = 1


def parts_of(cols):
    return [cols // 4, cols // 4, cols // 2]


def body(plane, field, start_one, start_two):
    rows, cols, depth = field.shape
    ny, nx, nz = plane
    planes = ny * nx
    splits = depth // 128
    part_ranks = RANK // 2 // (planes // splits)
    whole_rows = planes * cols
    half = whole_rows // 2
    parts = len(parts_of(cols))
    dma = pltpu.SemaphoreType.DMA
    vmem = pl.BlockSpec(memory_space=pltpu.VMEM)
    anywhere = pl.BlockSpec(memory_space=pl.ANY)
    core_shape = (RANK // 2, RANK // planes, depth)
    size = max(2 * rows, whole_rows)
    outs = pl.pallas_call(
        functools.partial(kernel, plane),
        out_shape=(
            jax.ShapeDtypeStruct((rows, RANK), f32),
            jax.ShapeDtypeStruct((cols, RANK), f32),
            jax.ShapeDtypeStruct(core_shape, f32),
        ),
        in_specs=[anywhere, anywhere, anywhere],
        out_specs=(anywhere, anywhere, anywhere),
        scratch_shapes=[
            pltpu.VMEM((cols, rows, depth), f32),
            pltpu.VMEM((cols // 2, rows, depth), f32),
            pltpu.VMEM((2 * rows, cols * depth), bf16),
            pltpu.VMEM((2 * rows, cols // 2 * depth), bf16),
            pltpu.VMEM((2 * rows, rows), f32),
            pltpu.VMEM((rows, rows), f32),
            pltpu.VMEM((rows // 2, rows), f32),
            pltpu.VMEM((3, size, size), bf16),
            pltpu.VMEM((RANK, size), f32),
            pltpu.VMEM((2, size, RANK), f32),
            pltpu.VMEM((2, RANK, size), f32),
            pltpu.VMEM((rows, RANK), f32),
            pltpu.VMEM((size, RANK), f32),
            pltpu.VMEM((RANK // 8, 9, 8, RANK), f32),
            pltpu.VMEM((cols, RANK, depth), f32),
            pltpu.VMEM((cols, RANK // 2, depth), f32),
            pltpu.VMEM((cols, RANK // 2, depth), f32),
            pltpu.VMEM((whole_rows, part_ranks, 128), f32),
            pltpu.VMEM((2 * whole_rows, part_ranks * 128), bf16),
            pltpu.VMEM((half, half), f32),
            pltpu.VMEM((half, half), f32),
            pltpu.VMEM((2, PACKED * half // 2, half // 2), f32),
            pltpu.VMEM((PACKED * half // 2, half // 2), f32),
            pltpu.VMEM((part_ranks, RANK, 128), f32),
            pltpu.VMEM(core_shape, f32),
            dma((cols,)),
            dma((2,)),
            dma((2, cols // 2)),
            dma((2,)),
            dma((2, 2)),
            dma((2, parts)),
            dma((2, parts, planes)),
            dma((2, CORE_PARTS, planes)),
            dma((3,)),
            *sum_scratch(plane, PACKED * rows // 2, rows // 2),
            *sum_scratch(plane, PACKED * half // 2, half // 2),
        ],
        compiler_params=pltpu.CompilerParams(collective_id=0, has_side_effects=True, vmem_limit_bytes=VMEM_LIMIT),
        name="hosvd",
    )(field, start_one, start_two)
    return pl.pallas_call(
        deliver,
        out_shape=tuple(jax.ShapeDtypeStruct(out.shape, f32) for out in outs),
        in_specs=[vmem] * len(outs),
        out_specs=(vmem,) * len(outs),
        name="deliver",
    )(*outs)


def solution(mesh):
    sizes = dict(mesh.shape)
    side = 4 if sizes["gy"] == 16 else 2
    plane = (sizes["gy"] // side, side, sizes["gz"])
    return jax.shard_map(
        functools.partial(body, plane),
        mesh=mesh,
        in_specs=(P("gx", "gy", "gz"), P(), P()),
        out_specs=(P("gx", None), P("gy", None), P("gx", "gy", "gz")),
        check_vma=False,
    )
```
